768 devices in a mesh: wide: 64 (over y, x, z_hi), narrow: 12 (over z_lo, core).
Axes of the slice: x: 4, y: 8, z: 12 (z_hi: 2, z_lo: 6; z = z_hi * 6 + z_lo), core: 2. Of those that a mesh axis runs over, the one named last changes fastest.
Arguments:
- hidden: bfloat16 [12, 16384, 5120], P('narrow', 'wide'), may hold values from -28 to 28
- segment: int32 [12, 16384], P('narrow', 'wide'), may hold values from 0 to 19, as said below
- grades: int32 [12, 4, 20], P('narrow'), may hold values from 0 to 4
- value_codes: bfloat16 [5120, 128], P('wide'), may hold values from -0.078125 to 0.078125
- value_scale: float32 [128], replicated, may hold values from 0.25 to 1.75
- output_codes: bfloat16 [5120, 128], P('wide'), may hold values from -0.5 to 0.5
- output_scale: bfloat16 [5120], P('wide'), may hold values from 0.25 to 1.75
- norm_gain: bfloat16 [5120], P('wide'), may hold values from 0.5 to 1.5
- final_gain: bfloat16 [5120], P('wide'), may hold values from 0.5 to 1.5
- score_vector: bfloat16 [5120], P('wide'), may hold values from -1 to 1
Outputs:
- value_grad: float32 [5120, 128], P('wide')
- output_grad: float32 [5120, 128], P('wide')
- list_loss: float32 [12, 4], P('narrow')
The draws below stay inside these ranges and needn't reach their ends.
Inputs may be any that keep to these rules, and one draw needn't show every extreme that they name: `segment`: within each list the candidate numbers never fall, and every candidate 0 to 19 holds 1 to 2048 tokens; one candidate of every list holds exactly 2048.
All inputs are finite; a program needn't handle non-finite values.
Results may differ from the reference program's by a relative error of at most 0.025.
Values may be sent and summed in bfloat16 or wider, within the bound.
No kernel may reach another device: no remote copies, remote signals or barrier semaphores. Data moves between devices by JAX's collectives and lax.ppermute only.
A program may use at most 64 MiB of HBM per device.

```python
import jax
import jax.numpy as jnp
from jax import lax

D = 5120
HD = 128
TOK_DEV = 256
CANDS = 20
LIST_LEN = 4096
GROUP_TOK = 16384
GROUP_LISTS = 4
LISTS = 48
TOKENS = 196608
N_WIDE = 64
N_NARROW = 12


def shared_direction(key):
    return jax.random.truncated_normal(jax.random.fold_in(key, 101), -2.5, 2.5, (D,), jnp.float32)


def draw_hidden(key, part):
    direction = shared_direction(key)
    key = jax.random.fold_in(key, 21)
    noise_key, pair_key, size_key, sign_key = jax.random.split(key, 4)
    shape = (N_NARROW, GROUP_TOK, D)
    noise = jax.random.truncated_normal(noise_key, -6.0, 6.0, shape, jnp.float32)
    pairing = jax.random.permutation(pair_key, jnp.arange(N_WIDE, dtype=jnp.int32))
    token_block = jnp.arange(GROUP_TOK, dtype=jnp.int32) // TOK_DEV
    feature_block = jnp.arange(D, dtype=jnp.int32) // (D // N_WIDE)
    paired = (pairing[token_block][:, None] == feature_block[None, :]).astype(jnp.float32)
    factor = 1.0 + 2.0 * paired
    magnitude = jax.random.uniform(size_key, (N_NARROW, GROUP_TOK, 1), jnp.float32, 0.2, 2.0)
    signs = (2 * jax.random.randint(sign_key, (N_NARROW, GROUP_TOK, 1), 0, 2, dtype=jnp.int32) - 1).astype(jnp.float32)
    along = magnitude * signs
    values = noise * factor[None, :, :] + along * direction[None, None, :]
    return values.astype(jnp.bfloat16)


def draw_score_vector(key, part):
    direction = shared_direction(key)
    return (direction * (45.0 / D)).astype(jnp.bfloat16)


def draw_segment(key, part):
    key = jax.random.fold_in(key, 11)
    most = LIST_LEN // 2
    rest = LIST_LEN - most
    keys = jax.random.split(key, N_NARROW * GROUP_LISTS)

    def one_list(list_key):
        cut_key, place_key = jax.random.split(list_key)
        cuts = jnp.sort(jax.random.permutation(cut_key, jnp.arange(1, rest, dtype=jnp.int32))[:CANDS - 2])
        edges = jnp.concatenate([jnp.zeros((1,), jnp.int32), cuts, jnp.full((1,), rest, jnp.int32)])
        pieces = edges[1:] - edges[:-1]
        where_most = jax.random.randint(place_key, (), 0, CANDS, dtype=jnp.int32)
        index = jnp.arange(CANDS, dtype=jnp.int32)
        source = jnp.clip(index - (index > where_most).astype(jnp.int32), 0, CANDS - 2)
        lengths = jnp.where(index == where_most, most, pieces[source])
        starts = jnp.cumsum(lengths)[:-1]
        position = jnp.arange(LIST_LEN, dtype=jnp.int32)
        return jnp.sum((position[:, None] >= starts[None, :]).astype(jnp.int32), axis=1)
    return jax.vmap(one_list)(keys).reshape(N_NARROW, GROUP_TOK).astype(jnp.int32)


def with_ends(values, rng, smallest, top_value):
    longest = values.shape.index(max(values.shape))
    spots = []
    for shift in (0, 1):
        where = [jax.random.randint(jax.random.fold_in(rng, axis), (), 0, length) for axis, length in enumerate(values.shape)]
        where[longest] = (where[longest] + shift) % values.shape[longest]
        spots.append(tuple(where))
    return values.at[spots[0]].set(smallest).at[spots[1]].set(top_value)


def block_scale(rng, extent, cuts, low, top_value):
    gain, own = 1.0, jax.random.fold_in(rng, 6)
    for dim, shards_of in cuts:
        draws = jnp.exp(jax.random.uniform(jax.random.fold_in(own, dim), (shards_of,), jnp.float32, low / len(cuts), top_value / len(cuts)))
        gain = gain * jnp.repeat(draws, extent[dim] // shards_of).reshape([-1 if axis == dim else 1 for axis in range(len(extent))])
    return gain


def bell_draw(key, dims, width, limit, shards=(), held_as=jnp.bfloat16):
    loudness = block_scale(key, dims, shards, -0.22, 0.18) if shards else 1.0
    values = jax.random.normal(key, dims, jnp.float32) * width * loudness
    return jnp.minimum(jnp.maximum(values, -limit), limit).astype(held_as)


def setup_inputs(seed: int = 0) -> dict:
    arg_keys = jax.random.split(jax.random.key(seed), 11)
    return {
        "hidden": draw_hidden(jax.random.fold_in(arg_keys[10], 71), 0),
        "segment": draw_segment(jax.random.fold_in(arg_keys[10], 71), 0),
        "grades": with_ends(jax.random.randint(arg_keys[2], (N_NARROW, GROUP_LISTS, CANDS), 0, 5), jax.random.fold_in(arg_keys[2], 1), 0, 4).astype(jnp.int32),
        "value_codes": bell_draw(arg_keys[3], (D, HD), D ** -0.5, 0.078125, ((0, 64),)),
        "value_scale": jnp.clip(1.0 + 0.15 * jax.random.normal(arg_keys[4], (HD,), jnp.float32), 0.25, 1.75),
        "output_codes": bell_draw(arg_keys[5], (D, HD), HD ** -0.5, 0.5, ((0, 64),)),
        "output_scale": jnp.clip(1.0 + 0.15 * jax.random.normal(arg_keys[6], (D,), jnp.float32), 0.25, 1.75).astype(jnp.bfloat16),
        "norm_gain": jnp.clip(1.0 + 0.1 * jax.random.normal(arg_keys[7], (D,), jnp.float32), 0.5, 1.5).astype(jnp.bfloat16),
        "final_gain": jnp.clip(1.0 + 0.1 * jax.random.normal(arg_keys[8], (D,), jnp.float32), 0.5, 1.5).astype(jnp.bfloat16),
        "score_vector": draw_score_vector(jax.random.fold_in(arg_keys[10], 71), 0),
    }


EPSILON = 1e-06
SOFT_CAP = 30.0

def forward_block(tokens, value_codes, value_scale, norm_gain):
    tokens32 = tokens.astype(jnp.float32)
    root_mean = jnp.sqrt(lax.optimization_barrier(jnp.mean(tokens32 * tokens32, axis=-1, keepdims=True)) + EPSILON)
    normed = (tokens32 / root_mean * norm_gain.astype(jnp.float32)).astype(jnp.bfloat16)
    value_half = (jnp.dot(normed, value_codes, preferred_element_type=jnp.float32) * value_scale).astype(jnp.bfloat16)
    return (tokens32, normed, value_half)

def residual_block(tokens32, value_half, output_codes, output_scale):
    branch = jnp.dot(value_half, output_codes.T, preferred_element_type=jnp.float32) * output_scale.astype(jnp.float32)
    return (tokens32 + branch).astype(jnp.bfloat16)

def score_terms(residual, final_gain, score_vector):
    resid32 = residual.astype(jnp.float32)
    final_root = jnp.sqrt(lax.optimization_barrier(jnp.mean(resid32 * resid32, axis=-1)) + EPSILON)
    weighted = final_gain.astype(jnp.float32) * score_vector.astype(jnp.float32)
    raw_score = lax.optimization_barrier(jnp.sum(resid32 * weighted, axis=-1)) / final_root
    capped = jnp.tanh(raw_score / SOFT_CAP)
    return (resid32, final_root, weighted, raw_score, capped)

def reference(hidden, segment, grades, value_codes, value_scale, output_codes, output_scale, norm_gain, final_gain, score_vector):
    block_count = TOKENS // TOK_DEV
    blocks = hidden.reshape(block_count, TOK_DEV, D)

    def first_pass(tokens):
        tokens32, normed, value_half = forward_block(tokens, value_codes, value_scale, norm_gain)
        residual = residual_block(tokens32, value_half, output_codes, output_scale)
        capped = score_terms(residual, final_gain, score_vector)[4]
        return (value_half, capped)
    halves, capped_all = lax.map(first_pass, blocks)
    token_score = (SOFT_CAP * capped_all).reshape(LISTS, LIST_LEN)
    seg = segment.reshape(LISTS, LIST_LEN)
    member = (seg[:, :, None] == jnp.arange(CANDS, dtype=jnp.int32)).astype(jnp.float32)
    counts = lax.optimization_barrier(jnp.sum(member, axis=1))
    cand_score = jnp.einsum('nlc,nl->nc', member, token_score) / counts
    teacher = grades.reshape(LISTS, CANDS).astype(jnp.float32)
    log_teacher = teacher - jnp.log(lax.optimization_barrier(jnp.sum(jnp.exp(teacher), axis=-1, keepdims=True)))
    log_student = cand_score - jnp.log(lax.optimization_barrier(jnp.sum(jnp.exp(cand_score), axis=-1, keepdims=True)))
    list_loss = lax.optimization_barrier(jnp.sum(jnp.exp(log_teacher) * (log_teacher - log_student), axis=-1))
    grad_cand = (jnp.exp(log_student) - jnp.exp(log_teacher)) / counts
    grad_base = jnp.einsum('nlc,nc->nl', member, grad_cand).reshape(block_count, TOK_DEV)

    def second_pass(carry, block):
        tokens, value_half, base = block
        tokens32 = tokens.astype(jnp.float32)
        root_mean = jnp.sqrt(lax.optimization_barrier(jnp.mean(tokens32 * tokens32, axis=-1, keepdims=True)) + EPSILON)
        normed = (tokens32 / root_mean * norm_gain.astype(jnp.float32)).astype(jnp.bfloat16)
        residual = residual_block(tokens32, value_half, output_codes, output_scale)
        resid32, final_root, weighted, raw_score, capped = score_terms(residual, final_gain, score_vector)
        grad_token = base * (1.0 - capped * capped)
        grad_resid = grad_token[:, None] * (weighted[None, :] / final_root[:, None] - resid32 * (raw_score / (D * final_root * final_root))[:, None])
        grad_branch = (grad_resid * output_scale.astype(jnp.float32)).astype(jnp.bfloat16)
        grad_values = (jnp.dot(grad_branch, output_codes, preferred_element_type=jnp.float32) * value_scale).astype(jnp.bfloat16)
        out_term = jnp.dot(grad_branch.T, value_half, preferred_element_type=jnp.float32)
        value_term = jnp.dot(normed.T, grad_values, preferred_element_type=jnp.float32)
        return ((carry[0] + value_term, carry[1] + out_term), None)
    zeros = jnp.zeros((D, HD), jnp.float32)
    (value_grad, output_grad), unused = lax.scan(second_pass, (zeros, zeros), (blocks, halves, grad_base))
    return (value_grad, output_grad, list_loss.reshape(N_NARROW, GROUP_LISTS))
```

```python
import jax
import jax.numpy as jnp
from jax import lax
from jax.sharding import Mesh, PartitionSpec as P

EPSILON = 1e-06
SOFT_CAP = 30.0
YX = ("yh", "yl", "x")
WIDE = ("yh", "yl", "x", "zh")
NARROW = ("zl", "c")
Z = ("zh", "zl")
SWAP = [(0, 1), (1, 0)]


def half_partner():
    pairs = []
    for z in range(12):
        to = (z + 3) % 12 if z % 6 >= 3 else (z - 3) % 12
        pairs.append((z, to))
    return pairs


def contract_rows(left, right):
    return lax.dot_general(
        left, right, (((0,), (0,)), ((), ())), preferred_element_type=jnp.float32
    )


def shards(
    hidden,
    segment,
    grades,
    value_codes,
    value_scale,
    output_codes,
    output_scale,
    norm_gain,
    final_gain,
    score_vector,
):
    rows, head_size = value_codes.shape
    core = lax.axis_index("c")
    z_half = lax.axis_index("zh")
    first = core == 0
    tokens32 = hidden[0].astype(jnp.float32)
    width = tokens32.shape[1]
    seg_local = segment[0]
    grade_rows = grades[0]
    group_lists, cand_count = grade_rows.shape

    with jax.named_scope("gather"):
        vectors = jnp.where(
            first, jnp.stack([norm_gain, output_scale]), jnp.stack([final_gain, score_vector])
        )
        vectors = jnp.pad(vectors, ((0, 6), (0, head_size - rows)))
        mine = jnp.concatenate([jnp.where(first, value_codes, output_codes), vectors], axis=0)
        other = lax.ppermute(mine, Z, half_partner())
        low = jnp.where(z_half == 0, mine, other)
        high = jnp.where(z_half == 0, other, mine)
        block = jnp.concatenate([low[:rows], high[:rows], low[rows : rows + 2], high[rows : rows + 6]], axis=0)
        spread = jnp.broadcast_to(block, (32,) + block.shape)
        own = lax.all_to_all(spread, YX, 0, 0)
        beside = lax.ppermute(own, "c", SWAP)
        value_block = jnp.where(first, own, beside)
        out_block = jnp.where(first, beside, own)
        value_full = value_block[:, : 2 * rows].reshape(width, head_size)
        out_full = out_block[:, : 2 * rows].reshape(width, head_size)

        def vector(block, which):
            parts = block[:, 2 * rows : 2 * rows + 4, :rows].reshape(32, 2, 2, rows)
            return parts[:, :, which].reshape(width).astype(jnp.float32)

        gain32 = vector(value_block, 0)
        scale32 = vector(value_block, 1)
        weighted = vector(out_block, 0) * vector(out_block, 1)

    root_mean = jnp.sqrt(jnp.mean(tokens32 * tokens32, axis=-1, keepdims=True) + EPSILON)
    normed = (tokens32 / root_mean * gain32).astype(jnp.bfloat16)
    mixed = jnp.dot(normed, value_full, preferred_element_type=jnp.float32)
    value_half = (mixed * value_scale).astype(jnp.bfloat16)
    branch = lax.dot_general(
        value_half, out_full, (((1,), (1,)), ((), ())), preferred_element_type=jnp.float32
    )
    residual = (tokens32 + branch * scale32).astype(jnp.bfloat16)
    resid32 = residual.astype(jnp.float32)
    final_root = jnp.sqrt(jnp.mean(resid32 * resid32, axis=-1) + EPSILON)
    raw_score = jnp.sum(resid32 * weighted, axis=-1) / final_root
    capped = jnp.tanh(raw_score / SOFT_CAP)
    token_score = SOFT_CAP * capped
    member = (seg_local[:, None] == jnp.arange(cand_count, dtype=jnp.int32)).astype(jnp.float32)

    with jax.named_scope("stats"):
        local = jnp.stack(
            [jnp.sum(token_score[:, None] * member, axis=0), jnp.sum(member, axis=0)]
        )
        local = jnp.pad(local, ((0, 6), (0, 128 - cand_count)))
        pair = local + lax.ppermute(local, "zh", SWAP)

    slope = 1.0 - capped * capped
    unit_resid = slope[:, None] * (
        weighted[None, :] / final_root[:, None]
        - resid32 * (raw_score / (width * final_root * final_root))[:, None]
    )
    unit_branch = (unit_resid * scale32).astype(jnp.bfloat16)
    unit_values = jnp.dot(unit_branch, out_full, preferred_element_type=jnp.float32) * value_scale

    with jax.named_scope("stats2"):
        spread = jnp.broadcast_to(pair, (8,) + pair.shape)
        stats = jnp.sum(lax.all_to_all(spread, ("yl", "x"), 0, 0), axis=0)
        sums, counts = stats[0, :cand_count], stats[1, :cand_count]
        cand_score = sums / counts
        teacher = lax.dynamic_index_in_dim(grade_rows, lax.axis_index("yh"), 0, keepdims=False)
        teacher = teacher.astype(jnp.float32)
        log_teacher = teacher - jnp.log(jnp.sum(jnp.exp(teacher)))
        log_student = cand_score - jnp.log(jnp.sum(jnp.exp(cand_score)))
        own_loss = jnp.sum(jnp.exp(log_teacher) * (log_teacher - log_student))
        grad_cand = (jnp.exp(log_student) - jnp.exp(log_teacher)) / counts
        factor = jnp.sum(member * grad_cand, axis=-1, keepdims=True)

    half_scaled = (factor * value_half.astype(jnp.float32)).astype(jnp.bfloat16)
    grad_values = (factor * unit_values).astype(jnp.bfloat16)
    output_term = contract_rows(unit_branch, half_scaled)
    value_term = contract_rows(normed, grad_values)

    with jax.named_scope("reduce"):
        keep = jnp.where(first, value_term, output_term)
        give = jnp.where(first, output_term, value_term).astype(jnp.bfloat16)
        got = lax.ppermute(give, "c", SWAP)
        both = (keep + got.astype(jnp.float32)).astype(jnp.bfloat16)
        loss_hi = own_loss.astype(jnp.bfloat16)
        loss_mid = own_loss - loss_hi.astype(jnp.float32)
        loss_lo = loss_mid.astype(jnp.bfloat16)
        loss_row = jnp.pad(jnp.stack([loss_hi, loss_lo])[None, :], ((0, 7), (0, head_size - 2)))
        sent = jnp.concatenate(
            [both.reshape(32, 2 * rows, head_size), jnp.broadcast_to(loss_row, (32, 8, head_size))],
            axis=1,
        )
        came = lax.all_to_all(sent, YX, 0, 0)
        part = jnp.sum(came[:, : 2 * rows].astype(jnp.float32), axis=0)
        losses = came.reshape(4, 8, 2 * rows + 8, head_size)[:, 0, 2 * rows, :2]
        list_loss = jnp.sum(losses.astype(jnp.float32), axis=-1)
        part = jnp.broadcast_to(part.reshape(2, 1, rows, head_size), (2, 6, rows, head_size))
        part = part.reshape(12, rows, head_size)
        total = jnp.sum(lax.all_to_all(part, Z, 0, 0), axis=0)
        pair = lax.all_gather(total, "c")
    return (pair[0], pair[1], list_loss[None, :])


def solution(mesh):
    grid = Mesh(mesh.devices.reshape(4, 2, 4, 2, 6, 2), WIDE + NARROW)
    in_specs = (
        P(NARROW, WIDE, None),
        P(NARROW, WIDE),
        P(NARROW, None, None),
        P(WIDE, None),
        P(),
        P(WIDE, None),
        P(WIDE),
        P(WIDE),
        P(WIDE),
        P(WIDE),
    )
    out_specs = (P(WIDE, None), P(WIDE, None), P(NARROW, None))
    return jax.shard_map(shards, mesh=grid, in_specs=in_specs, out_specs=out_specs, check_vma=False)
```

```python
import jax
import jax.numpy as jnp
from jax import lax
from jax.sharding import Mesh, PartitionSpec as P

EPSILON = 1e-06
SOFT_CAP = 30.0
YX = ("yh", "yl", "x")
WIDE = ("yh", "yl", "x", "zh")
NARROW = ("zl", "c")
Z = ("zh", "zl")
SWAP = [(0, 1), (1, 0)]


def half_partner():
    pairs = []
    for z in range(12):
        to = (z + 3) % 12 if z % 6 >= 3 else (z - 3) % 12
        pairs.append((z, to))
    return pairs


def contract_rows(left, right):
    return lax.dot_general(
        left, right, (((0,), (0,)), ((), ())), preferred_element_type=jnp.float32
    )


def shards(
    hidden,
    segment,
    grades,
    value_codes,
    value_scale,
    output_codes,
    output_scale,
    norm_gain,
    final_gain,
    score_vector,
):
    rows, head_size = value_codes.shape
    core = lax.axis_index("c")
    z_half = lax.axis_index("zh")
    first = core == 0
    tokens32 = hidden[0].astype(jnp.float32)
    width = tokens32.shape[1]
    seg_local = segment[0]
    grade_rows = grades[0]
    group_lists, cand_count = grade_rows.shape

    with jax.named_scope("gather"):
        vectors = jnp.where(
            first, jnp.stack([norm_gain, output_scale]), jnp.stack([final_gain, score_vector])
        )
        vectors = jnp.pad(vectors, ((0, 6), (0, head_size - rows)))
        mine = jnp.concatenate([jnp.where(first, value_codes, output_codes), vectors], axis=0)
        other = lax.ppermute(mine, Z, half_partner())
        low = jnp.where(z_half == 0, mine, other)
        high = jnp.where(z_half == 0, other, mine)
        block = jnp.concatenate([low[:rows], high[:rows], low[rows : rows + 2], high[rows : rows + 6]], axis=0)
        spread = jnp.broadcast_to(block, (32,) + block.shape)
        own = lax.all_to_all(spread, YX, 0, 0)
        beside = lax.ppermute(own, "c", SWAP)
        value_block = jnp.where(first, own, beside)
        out_block = jnp.where(first, beside, own)
        value_full = value_block[:, : 2 * rows].reshape(width, head_size)
        out_full = out_block[:, : 2 * rows].reshape(width, head_size)

        def vector(block, which):
            parts = block[:, 2 * rows : 2 * rows + 4, :rows].reshape(32, 2, 2, rows)
            return parts[:, :, which].reshape(width).astype(jnp.float32)

        gain32 = vector(value_block, 0)
        scale32 = vector(value_block, 1)
        weighted = vector(out_block, 0) * vector(out_block, 1)

    root_mean = jnp.sqrt(jnp.mean(tokens32 * tokens32, axis=-1, keepdims=True) + EPSILON)
    normed = (tokens32 / root_mean * gain32).astype(jnp.bfloat16)
    mixed = jnp.dot(normed, value_full, preferred_element_type=jnp.float32)
    value_half = (mixed * value_scale).astype(jnp.bfloat16)
    branch = lax.dot_general(
        value_half, out_full, (((1,), (1,)), ((), ())), preferred_element_type=jnp.float32
    )
    residual = (tokens32 + branch * scale32).astype(jnp.bfloat16)
    resid32 = residual.astype(jnp.float32)
    final_root = jnp.sqrt(jnp.mean(resid32 * resid32, axis=-1) + EPSILON)
    raw_score = jnp.sum(resid32 * weighted, axis=-1) / final_root
    capped = jnp.tanh(raw_score / SOFT_CAP)
    token_score = SOFT_CAP * capped
    member = (seg_local[:, None] == jnp.arange(cand_count, dtype=jnp.int32)).astype(jnp.float32)

    with jax.named_scope("stats"):
        local = jnp.stack(
            [jnp.sum(token_score[:, None] * member, axis=0), jnp.sum(member, axis=0)]
        )
        local = jnp.pad(local, ((0, 6), (0, 128 - cand_count)))
        spread = jnp.broadcast_to(local, (16,) + local.shape)
        arrived = lax.all_to_all(spread, ("yl", "x", "zh"), 0, 0)

    slope = 1.0 - capped * capped
    unit_resid = slope[:, None] * (
        weighted[None, :] / final_root[:, None]
        - resid32 * (raw_score / (width * final_root * final_root))[:, None]
    )
    unit_branch = (unit_resid * scale32).astype(jnp.bfloat16)
    unit_values = jnp.dot(unit_branch, out_full, preferred_element_type=jnp.float32) * value_scale

    with jax.named_scope("stats2"):
        stats = jnp.sum(arrived, axis=0)
        sums, counts = stats[0, :cand_count], stats[1, :cand_count]
        cand_score = sums / counts
        teacher = lax.dynamic_index_in_dim(grade_rows, lax.axis_index("yh"), 0, keepdims=False)
        teacher = teacher.astype(jnp.float32)
        log_teacher = teacher - jnp.log(jnp.sum(jnp.exp(teacher)))
        log_student = cand_score - jnp.log(jnp.sum(jnp.exp(cand_score)))
        own_loss = jnp.sum(jnp.exp(log_teacher) * (log_teacher - log_student))
        grad_cand = (jnp.exp(log_student) - jnp.exp(log_teacher)) / counts
        factor = jnp.sum(member * grad_cand, axis=-1, keepdims=True)

    half_scaled = (factor * value_half.astype(jnp.float32)).astype(jnp.bfloat16)
    grad_values = (factor * unit_values).astype(jnp.bfloat16)
    output_term = contract_rows(unit_branch, half_scaled)
    value_term = contract_rows(normed, grad_values)

    with jax.named_scope("reduce"):
        keep = jnp.where(first, value_term, output_term)
        give = jnp.where(first, output_term, value_term).astype(jnp.bfloat16)
        got = lax.ppermute(give, "c", SWAP)
        both = (keep + got.astype(jnp.float32)).astype(jnp.bfloat16)
        loss_hi = own_loss.astype(jnp.bfloat16)
        loss_mid = own_loss - loss_hi.astype(jnp.float32)
        loss_lo = loss_mid.astype(jnp.bfloat16)
        loss_row = jnp.pad(jnp.stack([loss_hi, loss_lo])[None, :], ((0, 7), (0, head_size - 2)))
        sent = jnp.concatenate(
            [both.reshape(32, 2 * rows, head_size), jnp.broadcast_to(loss_row, (32, 8, head_size))],
            axis=1,
        )
        came = lax.all_to_all(sent, YX, 0, 0)
        part = jnp.sum(came[:, : 2 * rows].astype(jnp.float32), axis=0)
        losses = came.reshape(4, 8, 2 * rows + 8, head_size)[:, 0, 2 * rows, :2]
        list_loss = jnp.sum(losses.astype(jnp.float32), axis=-1)
        part = part.astype(jnp.bfloat16).reshape(2, 1, rows, head_size)
        part = jnp.broadcast_to(part, (2, 6, rows, head_size)).reshape(12, rows, head_size)
        total = jnp.sum(lax.all_to_all(part, Z, 0, 0).astype(jnp.float32), axis=0)
        pair = lax.all_gather(total, "c")
    return (pair[0], pair[1], list_loss[None, :])


def solution(mesh):
    grid = Mesh(mesh.devices.reshape(4, 2, 4, 2, 6, 2), WIDE + NARROW)
    in_specs = (
        P(NARROW, WIDE, None),
        P(NARROW, WIDE),
        P(NARROW, None, None),
        P(WIDE, None),
        P(),
        P(WIDE, None),
        P(WIDE),
        P(WIDE),
        P(WIDE),
        P(WIDE),
    )
    out_specs = (P(WIDE, None), P(WIDE, None), P(NARROW, None))
    return jax.shard_map(shards, mesh=grid, in_specs=in_specs, out_specs=out_specs, check_vma=False)
```

```python
import jax
import jax.numpy as jnp
from jax import lax
from jax.experimental import pallas as pl
from jax.experimental.pallas import tpu as pltpu
from jax.sharding import Mesh, PartitionSpec as P

EPSILON = 1e-06
SOFT_CAP = 30.0
YX = ("yh", "yl", "x")
WIDE = ("yh", "yl", "x", "zh")
NARROW = ("zl", "c")
Z = ("zh", "zl")
SWAP = [(0, 1), (1, 0)]
LIST_DEVICES = 16
VMEM_LIMIT = 48 * 1024 * 1024
F32 = jnp.float32
BF16 = jnp.bfloat16


def half_partner():
    pairs = []
    for z in range(12):
        to = (z + 3) % 12 if z % 6 >= 3 else (z - 3) % 12
        pairs.append((z, to))
    return pairs


def lane_fold(x):
    total = x[:, :128]
    for k in range(1, x.shape[1] // 128):
        total = total + x[:, 128 * k : 128 * (k + 1)]
    return total


def forward_kernel(
    core_ref,
    hidden_ref,
    root_ref,
    own_ref,
    beside_ref,
    gain_ref,
    scale_ref,
    weighted_ref,
    value_scale_ref,
    segment_ref,
    normed_ref,
    resid_ref,
    out_ref,
    half_ref,
    columns_ref,
    stats_ref,
    value_ref,
):
    blocks, _, _ = own_ref.shape
    tokens, width = hidden_ref.shape
    per = width // blocks
    tile = 4 * per

    def place(value_from, out_from):
        for k in range(blocks):
            value_ref[per * k : per * (k + 1), :] = value_from[k, :per, :]
            out_ref[per * k : per * (k + 1), :] = out_from[k, :per, :]

    @pl.when(core_ref[0] == 0)
    def _():
        place(own_ref, beside_ref)

    @pl.when(core_ref[0] != 0)
    def _():
        place(beside_ref, own_ref)

    inverse = 1.0 / root_ref[...]
    mixed = jnp.zeros((tokens, value_ref.shape[1]), F32)
    for j in range(width // tile):
        span = slice(tile * j, tile * (j + 1))
        scaled = hidden_ref[:, span].astype(F32) * inverse
        normed = (scaled * gain_ref[:, span]).astype(BF16)
        normed_ref[:, span] = normed
        mixed = mixed + jnp.dot(normed, value_ref[span, :], preferred_element_type=F32)
    value_half = (mixed * value_scale_ref[...]).astype(BF16)
    half_ref[...] = value_half
    squares = jnp.zeros((tokens, 128), F32)
    scores = jnp.zeros((tokens, 128), F32)
    for j in range(width // tile):
        span = slice(tile * j, tile * (j + 1))
        branch = lax.dot_general(
            value_half, out_ref[span, :], (((1,), (1,)), ((), ())), preferred_element_type=F32
        )
        residual = (hidden_ref[:, span].astype(F32) + branch * scale_ref[:, span]).astype(BF16)
        resid_ref[:, span] = residual
        resid32 = residual.astype(F32)
        squares = squares + lane_fold(resid32 * resid32)
        scores = scores + lane_fold(resid32 * weighted_ref[:, span])
    final_root = jnp.sqrt(jnp.sum(squares, axis=1, keepdims=True) / width + EPSILON)
    raw_score = jnp.sum(scores, axis=1, keepdims=True) / final_root
    capped = jnp.tanh(raw_score / SOFT_CAP)
    slope = 1.0 - capped * capped
    lead = slope / final_root
    pull = slope * raw_score / (width * final_root * final_root)
    lanes = lax.broadcasted_iota(jnp.int32, (tokens, 128), 1)
    columns_ref[...] = jnp.where(lanes == 0, lead, pull)
    member = segment_ref[...] == lanes
    sums = jnp.sum(jnp.where(member, SOFT_CAP * capped, 0.0), axis=0, keepdims=True)
    counts = jnp.sum(jnp.where(member, 1.0, 0.0), axis=0, keepdims=True)
    row = lax.broadcasted_iota(jnp.int32, (8, 128), 0)
    packed = jnp.where(row == 0, sums, counts)
    for k in range(stats_ref.shape[0]):
        stats_ref[k] = packed


def backward_kernel(
    resid_ref, out_ref, columns_ref, scale_ref, weighted_ref, value_scale_ref, unit_ref, values_ref
):
    tokens, width = resid_ref.shape
    tile = 640
    lead = columns_ref[:, 0:1]
    pull = columns_ref[:, 1:2]
    total = jnp.zeros(values_ref.shape, F32)
    for j in range(width // tile):
        span = slice(tile * j, tile * (j + 1))
        slope = lead * weighted_ref[:, span] - pull * resid_ref[:, span].astype(F32)
        unit = (slope * scale_ref[:, span]).astype(BF16)
        unit_ref[:, span] = unit
        total = total + jnp.dot(unit, out_ref[span, :], preferred_element_type=F32)
    values_ref[...] = total * value_scale_ref[...]


def term_kernel(pick_ref, normed_ref, unit_ref, values_ref, half_ref, factor_ref, term_ref, small_ref):
    @pl.when(pl.program_id(0) == 0)
    def _():
        side = jnp.where(pick_ref[0] == 0, values_ref[...], half_ref[...].astype(F32))
        small_ref[...] = (factor_ref[...] * side).T.astype(BF16)

    def fill(tall_ref):
        term = jnp.dot(small_ref[...], tall_ref[...], preferred_element_type=F32)
        term_ref[...] = term.T.astype(term_ref.dtype)

    @pl.when(pick_ref[0] == 0)
    def _():
        fill(normed_ref)

    @pl.when(pick_ref[0] != 0)
    def _():
        fill(unit_ref)


def run_forward(core, hidden, root, own, beside, gain, scale, weighted, value_scale, segment):
    tokens, width = hidden.shape
    head = value_scale.shape[1]
    shape = jax.ShapeDtypeStruct
    vmem = pl.BlockSpec(memory_space=pltpu.VMEM)
    return pl.pallas_call(
        forward_kernel,
        out_shape=(
            shape((tokens, width), BF16),
            shape((tokens, width), BF16),
            shape((width, head), BF16),
            shape((tokens, head), BF16),
            shape((tokens, 128), F32),
            shape((LIST_DEVICES, 8, 128), F32),
        ),
        in_specs=[pl.BlockSpec(memory_space=pltpu.SMEM)] + [vmem] * 9,
        out_specs=(vmem,) * 6,
        scratch_shapes=[pltpu.VMEM((width, head), BF16)],
        compiler_params=pltpu.CompilerParams(vmem_limit_bytes=VMEM_LIMIT),
        cost_estimate=pl.CostEstimate(
            flops=4 * tokens * width * head, bytes_accessed=12 * width * tokens, transcendentals=tokens
        ),
        name="forward",
    )(core, hidden, root, own, beside, gain, scale, weighted, value_scale, segment)


def run_backward(resid, out_full, columns, scale, weighted, value_scale):
    tokens, width = resid.shape
    head = value_scale.shape[1]
    vmem = pl.BlockSpec(memory_space=pltpu.VMEM)
    return pl.pallas_call(
        backward_kernel,
        out_shape=(
            jax.ShapeDtypeStruct((tokens, width), BF16),
            jax.ShapeDtypeStruct((tokens, head), F32),
        ),
        in_specs=[vmem] * 6,
        out_specs=(vmem,) * 2,
        compiler_params=pltpu.CompilerParams(vmem_limit_bytes=VMEM_LIMIT),
        cost_estimate=pl.CostEstimate(
            flops=2 * tokens * width * head, bytes_accessed=8 * width * tokens, transcendentals=0
        ),
        name="backward",
    )(resid, out_full, columns, scale, weighted, value_scale)


def run_term(pick, normed, unit, values, half, factor, dtype):
    tokens, width = normed.shape
    head = values.shape[1]
    tile = 1280
    whole = lambda j, pick: (0, 0)
    return pl.pallas_call(
        term_kernel,
        out_shape=jax.ShapeDtypeStruct((width, head), dtype),
        grid_spec=pltpu.PrefetchScalarGridSpec(
            num_scalar_prefetch=1,
            grid=(width // tile,),
            in_specs=[
                pl.BlockSpec((tokens, tile), lambda j, pick: (0, j * (1 - pick[0]))),
                pl.BlockSpec((tokens, tile), lambda j, pick: (0, j * pick[0])),
                pl.BlockSpec((tokens, head), whole),
                pl.BlockSpec((tokens, head), whole),
                pl.BlockSpec((tokens, 1), whole),
            ],
            out_specs=pl.BlockSpec((tile, head), lambda j, pick: (j, 0)),
            scratch_shapes=[pltpu.VMEM((head, tokens), BF16)],
        ),
        compiler_params=pltpu.CompilerParams(vmem_limit_bytes=VMEM_LIMIT),
        cost_estimate=pl.CostEstimate(
            flops=2 * tokens * width * head, bytes_accessed=4 * width * tokens, transcendentals=0
        ),
        name="term",
    )(pick, normed, unit, values, half, factor)


def shards(
    hidden,
    segment,
    grades,
    value_codes,
    value_scale,
    output_codes,
    output_scale,
    norm_gain,
    final_gain,
    score_vector,
):
    rows, head_size = value_codes.shape
    core = lax.axis_index("c")
    z_half = lax.axis_index("zh")
    first = core == 0
    tokens = hidden[0]
    width = tokens.shape[1]
    seg_local = segment[0][:, None]
    grade_rows = grades[0]
    cand_count = grade_rows.shape[1]

    with jax.named_scope("gather"):
        vectors = jnp.where(
            first, jnp.stack([norm_gain, output_scale]), jnp.stack([final_gain, score_vector])
        )
        vectors = jnp.pad(vectors, ((0, 6), (0, head_size - rows)))
        mine = jnp.concatenate([jnp.where(first, value_codes, output_codes), vectors], axis=0)
        other = lax.ppermute(mine, Z, half_partner())
        low = jnp.where(z_half == 0, mine, other)
        high = jnp.where(z_half == 0, other, mine)
        block = jnp.concatenate([low[:rows], high[:rows], low[rows : rows + 2], high[rows : rows + 6]], axis=0)
        spread = jnp.broadcast_to(block, (32,) + block.shape)
        own = lax.all_to_all(spread, YX, 0, 0)
        tokens32 = tokens.astype(F32)
        root = jnp.sqrt(jnp.mean(tokens32 * tokens32, axis=-1, keepdims=True) + EPSILON)
        own, root = lax.optimization_barrier((own, root))
        beside = lax.ppermute(own, "c", SWAP)

        def vector(block, which):
            parts = block[:, 2 * rows : 2 * rows + 4, :rows].reshape(32, 2, 2, rows)
            return parts[:, :, which].reshape(1, width).astype(F32)

        gain32 = jnp.where(first, vector(own, 0), vector(beside, 0))
        scale32 = jnp.where(first, vector(own, 1), vector(beside, 1))
        final32 = jnp.where(first, vector(beside, 0), vector(own, 0))
        score32 = jnp.where(first, vector(beside, 1), vector(own, 1))
        weighted = final32 * score32

    value_row = value_scale[None, :]
    pick = core.astype(jnp.int32)[None]
    normed, resid, out_full, value_half, columns, stats = run_forward(
        pick, tokens, root, own, beside, gain32, scale32, weighted, value_row, seg_local
    )
    with jax.named_scope("stats"):
        arrived = lax.all_to_all(stats, ("yl", "x", "zh"), 0, 0)

    unit, values = run_backward(resid, out_full, columns, scale32, weighted, value_row)

    with jax.named_scope("factor"):
        stats = jnp.sum(arrived, axis=0)
        sums, counts = stats[0, :cand_count], stats[1, :cand_count]
        cand_score = sums / counts
        teacher = lax.dynamic_index_in_dim(grade_rows, lax.axis_index("yh"), 0, keepdims=False)
        teacher = teacher.astype(F32)
        log_teacher = teacher - jnp.log(jnp.sum(jnp.exp(teacher)))
        log_student = cand_score - jnp.log(jnp.sum(jnp.exp(cand_score)))
        own_loss = jnp.sum(jnp.exp(log_teacher) * (log_teacher - log_student))
        grad_cand = (jnp.exp(log_student) - jnp.exp(log_teacher)) / counts
        member = (seg_local == jnp.arange(cand_count, dtype=jnp.int32)).astype(F32)
        factor = jnp.sum(member * grad_cand, axis=-1, keepdims=True)

    give = run_term(1 - pick, normed, unit, values, value_half, factor, BF16)
    with jax.named_scope("reduce"):
        got = lax.ppermute(give, "c", SWAP)
        keep = run_term(pick, normed, unit, values, value_half, factor, F32)
        both = (keep + got.astype(F32)).astype(BF16)
        loss_hi = own_loss.astype(BF16)
        loss_lo = (own_loss - loss_hi.astype(F32)).astype(BF16)
        loss_row = jnp.pad(jnp.stack([loss_hi, loss_lo])[None, :], ((0, 7), (0, head_size - 2)))
        sent = jnp.concatenate(
            [both.reshape(32, 2 * rows, head_size), jnp.broadcast_to(loss_row, (32, 8, head_size))],
            axis=1,
        )
        came = lax.all_to_all(sent, YX, 0, 0)
        part = jnp.sum(came[:, : 2 * rows].astype(F32), axis=0)
        losses = came.reshape(4, 8, 2 * rows + 8, head_size)[:, 0, 2 * rows, :2]
        list_loss = jnp.sum(losses.astype(F32), axis=-1)
        part = part.astype(BF16).reshape(2, 1, rows, head_size)
        part = jnp.broadcast_to(part, (2, 6, rows, head_size)).reshape(12, rows, head_size)
        total = jnp.sum(lax.all_to_all(part, Z, 0, 0).astype(F32), axis=0)
        pair = lax.all_gather(total, "c")
    return (pair[0], pair[1], list_loss[None, :])


def solution(mesh):
    grid = Mesh(mesh.devices.reshape(4, 2, 4, 2, 6, 2), WIDE + NARROW)
    in_specs = (
        P(NARROW, WIDE, None),
        P(NARROW, WIDE),
        P(NARROW, None, None),
        P(WIDE, None),
        P(),
        P(WIDE, None),
        P(WIDE),
        P(WIDE),
        P(WIDE),
        P(WIDE),
    )
    out_specs = (P(WIDE, None), P(WIDE, None), P(NARROW, None))
    return jax.shard_map(shards, mesh=grid, in_specs=in_specs, out_specs=out_specs, check_vma=False)
```

```python
import jax
import jax.numpy as jnp
from jax import lax
from jax.experimental import pallas as pl
from jax.experimental.pallas import tpu as pltpu
from jax.sharding import Mesh, PartitionSpec as P

EPSILON = 1e-06
SOFT_CAP = 30.0
Y = ("yh", "yl")
WIDE = ("yh", "yl", "x", "zh")
NARROW = ("za", "zb", "c")
Z = ("zh", "za", "zb")
XB = ("x", "zb")
SWAP = [(0, 1), (1, 0)]
LIST_DEVICES = 16
VMEM_LIMIT = 48 * 1024 * 1024
F32 = jnp.float32
BF16 = jnp.bfloat16


def half_partner():
    pairs = []
    for z in range(12):
        if z // 6 != z % 2:
            pairs.append((z, (z + 3) % 12 if z % 6 >= 3 else (z - 3) % 12))
    return pairs


def place(source_ref, rows, target_ref):
    pairs, ys = source_ref.shape[0], source_ref.shape[1]
    for y in range(ys):
        for k in range(pairs):
            at = rows * (y * pairs + k)
            target_ref[at : at + rows, :] = source_ref[k, y, :rows, :]


def lane_fold(x):
    total = x[:, :128]
    for k in range(1, x.shape[1] // 128):
        total = total + x[:, 128 * k : 128 * (k + 1)]
    return total


def forward_kernel(
    core_ref,
    hidden_ref,
    root_ref,
    own_ref,
    beside_ref,
    gain_ref,
    scale_ref,
    weighted_ref,
    value_scale_ref,
    segment_ref,
    normed_ref,
    resid_ref,
    half_ref,
    columns_ref,
    stats_ref,
    value_ref,
    out_ref,
):
    tokens, width = hidden_ref.shape
    rows = width // (own_ref.shape[0] * own_ref.shape[1])
    tile = 640

    @pl.when(core_ref[0] == 0)
    def _():
        place(own_ref, rows, value_ref)
        place(beside_ref, rows, out_ref)

    @pl.when(core_ref[0] != 0)
    def _():
        place(beside_ref, rows, value_ref)
        place(own_ref, rows, out_ref)

    inverse = 1.0 / root_ref[...]
    mixed = jnp.zeros((tokens, value_ref.shape[1]), F32)
    for j in range(width // tile):
        span = slice(tile * j, tile * (j + 1))
        scaled = hidden_ref[:, span].astype(F32) * inverse
        normed = (scaled * gain_ref[:, span]).astype(BF16)
        normed_ref[:, span] = normed
        mixed = mixed + jnp.dot(normed, value_ref[span, :], preferred_element_type=F32)
    value_half = (mixed * value_scale_ref[...]).astype(BF16)
    half_ref[...] = value_half
    squares = jnp.zeros((tokens, 128), F32)
    scores = jnp.zeros((tokens, 128), F32)
    for j in range(width // tile):
        span = slice(tile * j, tile * (j + 1))
        branch = lax.dot_general(
            value_half, out_ref[span, :], (((1,), (1,)), ((), ())), preferred_element_type=F32
        )
        residual = (hidden_ref[:, span].astype(F32) + branch * scale_ref[:, span]).astype(BF16)
        resid_ref[:, span] = residual
        resid32 = residual.astype(F32)
        squares = squares + lane_fold(resid32 * resid32)
        scores = scores + lane_fold(resid32 * weighted_ref[:, span])
    final_root = jnp.sqrt(jnp.sum(squares, axis=1, keepdims=True) / width + EPSILON)
    raw_score = jnp.sum(scores, axis=1, keepdims=True) / final_root
    capped = jnp.tanh(raw_score / SOFT_CAP)
    slope = 1.0 - capped * capped
    lead = slope / final_root
    pull = slope * raw_score / (width * final_root * final_root)
    lanes = lax.broadcasted_iota(jnp.int32, (tokens, 128), 1)
    columns_ref[...] = jnp.where(lanes == 0, lead, pull)
    member = segment_ref[...] == lanes
    sums = jnp.sum(jnp.where(member, SOFT_CAP * capped, 0.0), axis=0, keepdims=True)
    counts = jnp.sum(jnp.where(member, 1.0, 0.0), axis=0, keepdims=True)
    row = lax.broadcasted_iota(jnp.int32, (8, 128), 0)
    packed = jnp.where(row == 0, sums, counts)
    for k in range(stats_ref.shape[0]):
        stats_ref[k] = packed


def backward_kernel(
    core_ref,
    resid_ref,
    own_ref,
    beside_ref,
    columns_ref,
    scale_ref,
    weighted_ref,
    value_scale_ref,
    unit_ref,
    values_ref,
    out_ref,
):
    tokens, width = resid_ref.shape
    rows = width // (own_ref.shape[0] * own_ref.shape[1])
    tile = 640

    @pl.when(core_ref[0] == 0)
    def _():
        place(beside_ref, rows, out_ref)

    @pl.when(core_ref[0] != 0)
    def _():
        place(own_ref, rows, out_ref)

    lead = columns_ref[:, 0:1]
    pull = columns_ref[:, 1:2]
    total = jnp.zeros(values_ref.shape, F32)
    for j in range(width // tile):
        span = slice(tile * j, tile * (j + 1))
        slope = lead * weighted_ref[:, span] - pull * resid_ref[:, span].astype(F32)
        unit = (slope * scale_ref[:, span]).astype(BF16)
        unit_ref[:, span] = unit
        total = total + jnp.dot(unit, out_ref[span, :], preferred_element_type=F32)
    values_ref[...] = total * value_scale_ref[...]


def term_kernel(pick_ref, normed_ref, unit_ref, values_ref, half_ref, factor_ref, term_ref, small_ref):
    @pl.when(pl.program_id(0) == 0)
    def _():
        side = jnp.where(pick_ref[0] == 0, values_ref[...], half_ref[...].astype(F32))
        small_ref[...] = (factor_ref[...] * side).T.astype(BF16)

    def fill(tall_ref):
        term = jnp.dot(small_ref[...], tall_ref[...], preferred_element_type=F32)
        term_ref[...] = term.T.astype(term_ref.dtype)

    @pl.when(pick_ref[0] == 0)
    def _():
        fill(normed_ref)

    @pl.when(pick_ref[0] != 0)
    def _():
        fill(unit_ref)


def run_forward(core, hidden, root, own, beside, gain, scale, weighted, value_scale, segment):
    tokens, width = hidden.shape
    head = value_scale.shape[1]
    shape = jax.ShapeDtypeStruct
    vmem = pl.BlockSpec(memory_space=pltpu.VMEM)
    return pl.pallas_call(
        forward_kernel,
        out_shape=(
            shape((tokens, width), BF16),
            shape((tokens, width), BF16),
            shape((tokens, head), BF16),
            shape((tokens, 128), F32),
            shape((LIST_DEVICES, 8, 128), F32),
        ),
        in_specs=[pl.BlockSpec(memory_space=pltpu.SMEM)] + [vmem] * 9,
        out_specs=(vmem,) * 5,
        scratch_shapes=[pltpu.VMEM((width, head), BF16), pltpu.VMEM((width, head), BF16)],
        compiler_params=pltpu.CompilerParams(vmem_limit_bytes=VMEM_LIMIT),
        cost_estimate=pl.CostEstimate(
            flops=4 * tokens * width * head, bytes_accessed=12 * width * tokens, transcendentals=tokens
        ),
        name="forward",
    )(core, hidden, root, own, beside, gain, scale, weighted, value_scale, segment)


def run_backward(core, resid, own, beside, columns, scale, weighted, value_scale):
    tokens, width = resid.shape
    head = value_scale.shape[1]
    vmem = pl.BlockSpec(memory_space=pltpu.VMEM)
    return pl.pallas_call(
        backward_kernel,
        out_shape=(
            jax.ShapeDtypeStruct((tokens, width), BF16),
            jax.ShapeDtypeStruct((tokens, head), F32),
        ),
        in_specs=[pl.BlockSpec(memory_space=pltpu.SMEM)] + [vmem] * 7,
        out_specs=(vmem,) * 2,
        scratch_shapes=[pltpu.VMEM((width, head), BF16)],
        compiler_params=pltpu.CompilerParams(vmem_limit_bytes=VMEM_LIMIT),
        cost_estimate=pl.CostEstimate(
            flops=2 * tokens * width * head, bytes_accessed=8 * width * tokens, transcendentals=0
        ),
        name="backward",
    )(core, resid, own, beside, columns, scale, weighted, value_scale)


def run_term(pick, normed, unit, values, half, factor, dtype):
    tokens, width = normed.shape
    head = values.shape[1]
    tile = 1280
    whole = lambda j, pick: (0, 0)
    return pl.pallas_call(
        term_kernel,
        out_shape=jax.ShapeDtypeStruct((width, head), dtype),
        grid_spec=pltpu.PrefetchScalarGridSpec(
            num_scalar_prefetch=1,
            grid=(width // tile,),
            in_specs=[
                pl.BlockSpec((tokens, tile), lambda j, pick: (0, j * (1 - pick[0]))),
                pl.BlockSpec((tokens, tile), lambda j, pick: (0, j * pick[0])),
                pl.BlockSpec((tokens, head), whole),
                pl.BlockSpec((tokens, head), whole),
                pl.BlockSpec((tokens, 1), whole),
            ],
            out_specs=pl.BlockSpec((tile, head), lambda j, pick: (j, 0)),
            scratch_shapes=[pltpu.VMEM((head, tokens), BF16)],
        ),
        compiler_params=pltpu.CompilerParams(vmem_limit_bytes=VMEM_LIMIT),
        cost_estimate=pl.CostEstimate(
            flops=2 * tokens * width * head, bytes_accessed=4 * width * tokens, transcendentals=0
        ),
        name="term",
    )(pick, normed, unit, values, half, factor)


def shards(
    hidden,
    segment,
    grades,
    value_codes,
    value_scale,
    output_codes,
    output_scale,
    norm_gain,
    final_gain,
    score_vector,
):
    rows, head_size = value_codes.shape
    core = lax.axis_index("c")
    first = core == 0
    tokens = hidden[0]
    width = tokens.shape[1]
    seg_local = segment[0][:, None]
    grade_rows = grades[0]
    cand_count = grade_rows.shape[1]

    with jax.named_scope("gather"):
        vectors = jnp.where(
            first, jnp.stack([norm_gain, output_scale]), jnp.stack([final_gain, score_vector])
        )
        vectors = jnp.pad(vectors, ((0, 6), (0, head_size - rows)))
        mine = jnp.concatenate([jnp.where(first, value_codes, output_codes), vectors], axis=0)
        other = lax.ppermute(mine, Z, half_partner())
        block = jnp.where(lax.axis_index("zh") == lax.axis_index("zb"), mine, other)
        column = lax.all_to_all(jnp.broadcast_to(block, (8,) + block.shape), Y, 0, 0)
        spread = jnp.broadcast_to(column, (8,) + column.shape)
        own = lax.all_to_all(spread, XB, 0, 0)
        tokens32 = tokens.astype(F32)
        root = jnp.sqrt(jnp.mean(tokens32 * tokens32, axis=-1, keepdims=True) + EPSILON)
        own, root = lax.optimization_barrier((own, root))
        beside = lax.ppermute(own, "c", SWAP)

        def vector(block, which):
            parts = block[:, :, rows + which, :rows]
            return jnp.swapaxes(parts, 0, 1).reshape(1, width).astype(F32)

        gain32 = jnp.where(first, vector(own, 0), vector(beside, 0))
        scale32 = jnp.where(first, vector(own, 1), vector(beside, 1))
        final32 = jnp.where(first, vector(beside, 0), vector(own, 0))
        score32 = jnp.where(first, vector(beside, 1), vector(own, 1))
        weighted = final32 * score32

    value_row = value_scale[None, :]
    pick = core.astype(jnp.int32)[None]
    normed, resid, value_half, columns, stats = run_forward(
        pick, tokens, root, own, beside, gain32, scale32, weighted, value_row, seg_local
    )
    with jax.named_scope("stats"):
        arrived = lax.all_to_all(stats, ("yl", "x", "zh"), 0, 0)

    unit, values = run_backward(pick, resid, own, beside, columns, scale32, weighted, value_row)

    with jax.named_scope("factor"):
        stats = jnp.sum(arrived, axis=0)
        sums, counts = stats[0, :cand_count], stats[1, :cand_count]
        cand_score = sums / counts
        teacher = lax.dynamic_index_in_dim(grade_rows, lax.axis_index("yh"), 0, keepdims=False)
        teacher = teacher.astype(F32)
        log_teacher = teacher - jnp.log(jnp.sum(jnp.exp(teacher)))
        log_student = cand_score - jnp.log(jnp.sum(jnp.exp(cand_score)))
        own_loss = jnp.sum(jnp.exp(log_teacher) * (log_teacher - log_student))
        grad_cand = (jnp.exp(log_student) - jnp.exp(log_teacher)) / counts
        member = (seg_local == jnp.arange(cand_count, dtype=jnp.int32)).astype(F32)
        factor = jnp.sum(member * grad_cand, axis=-1, keepdims=True)

    give = run_term(1 - pick, normed, unit, values, value_half, factor, BF16)
    with jax.named_scope("reduce"):
        got = lax.ppermute(give, "c", SWAP)
        keep = run_term(pick, normed, unit, values, value_half, factor, F32)
        both = (keep + got.astype(F32)).astype(BF16)
        loss_hi = own_loss.astype(BF16)
        loss_lo = (own_loss - loss_hi.astype(F32)).astype(BF16)
        loss_row = jnp.pad(jnp.stack([loss_hi, loss_lo])[None, :], ((0, 7), (0, head_size - 2)))
        half = rows // 2
        sent = both.reshape(8, 4, 2, 2, half, head_size).transpose(1, 3, 0, 2, 4, 5)
        came = lax.all_to_all(sent.reshape(8, 8 * rows, head_size), XB, 0, 0)
        part = jnp.sum(came.astype(F32), axis=0).astype(BF16).reshape(8, rows, head_size)
        part = jnp.concatenate([part, jnp.broadcast_to(loss_row, (8, 8, head_size))], axis=1)
        came = lax.all_to_all(part, Y, 0, 0)
        losses = came.reshape(4, 2, rows + 8, head_size)[:, 0, rows, :2]
        list_loss = jnp.sum(losses.astype(F32), axis=-1)
        part = jnp.sum(came[:, :rows].astype(F32), axis=0).astype(BF16)
        part = part.reshape(2, 1, half, head_size)
        part = jnp.broadcast_to(part, (2, 6, half, head_size)).reshape(12, half, head_size)
        came = lax.all_to_all(part, Z, 0, 0).astype(F32)
        total = jnp.sum(came.reshape(6, 2, half, head_size), axis=0).reshape(rows, head_size)
        pair = lax.all_gather(total, "c")
    return (pair[0], pair[1], list_loss[None, :])


def solution(mesh):
    grid = Mesh(mesh.devices.reshape(4, 2, 4, 2, 3, 2, 2), WIDE + NARROW)
    in_specs = (
        P(NARROW, WIDE, None),
        P(NARROW, WIDE),
        P(NARROW, None, None),
        P(WIDE, None),
        P(),
        P(WIDE, None),
        P(WIDE),
        P(WIDE),
        P(WIDE),
        P(WIDE),
    )
    out_specs = (P(WIDE, None), P(WIDE, None), P(NARROW, None))
    return jax.shard_map(shards, mesh=grid, in_specs=in_specs, out_specs=out_specs, check_vma=False)
```

```python
import jax
import jax.numpy as jnp
from jax import lax
from jax.experimental import pallas as pl
from jax.experimental.pallas import tpu as pltpu
from jax.sharding import Mesh, PartitionSpec as P

EPSILON = 1e-06
SOFT_CAP = 30.0
Y = ("yh", "yl")
WIDE = ("yh", "yl", "x", "zh")
NARROW = ("za", "zb", "c")
Z = ("zh", "za", "zb")
XB = ("x", "zb")
SWAP = [(0, 1), (1, 0)]
LIST_DEVICES = 16
VMEM_LIMIT = 48 * 1024 * 1024
TERM_LIMIT = 16 * 1024 * 1024
F32 = jnp.float32
BF16 = jnp.bfloat16


def half_partner():
    pairs = []
    for z in range(12):
        if z // 6 != z % 2:
            pairs.append((z, (z + 3) % 12 if z % 6 >= 3 else (z - 3) % 12))
    return pairs


def place(source_ref, rows, target_ref):
    pairs, ys = source_ref.shape[0], source_ref.shape[1]
    for y in range(ys):
        for k in range(pairs):
            at = rows * (y * pairs + k)
            target_ref[at : at + rows, :] = source_ref[k, y, :rows, :]


def lane_fold(x):
    total = x[:, :128]
    for k in range(1, x.shape[1] // 128):
        total = total + x[:, 128 * k : 128 * (k + 1)]
    return total


def forward_kernel(
    core_ref,
    hidden_ref,
    root_ref,
    own_ref,
    beside_ref,
    gain_ref,
    scale_ref,
    weighted_ref,
    value_scale_ref,
    segment_ref,
    normed_out,
    resid_out,
    half_ref,
    columns_ref,
    stats_ref,
    value_ref,
    out_ref,
    normed_ref,
    resid_ref,
    sems,
):
    tokens, width = hidden_ref.shape
    rows = width // (own_ref.shape[0] * own_ref.shape[1])
    tile = 640

    @pl.when(core_ref[0] == 0)
    def _():
        place(own_ref, rows, value_ref)
        place(beside_ref, rows, out_ref)

    @pl.when(core_ref[0] != 0)
    def _():
        place(beside_ref, rows, value_ref)
        place(own_ref, rows, out_ref)

    copies = []
    inverse = 1.0 / root_ref[...]
    mixed = jnp.zeros((tokens, value_ref.shape[1]), F32)
    for j in range(width // tile):
        span = slice(tile * j, tile * (j + 1))
        scaled = hidden_ref[:, span].astype(F32) * inverse
        normed = (scaled * gain_ref[:, span]).astype(BF16)
        normed_ref[:, span] = normed
        copies.append(pltpu.make_async_copy(normed_ref.at[:, span], normed_out.at[:, span], sems.at[0, j]))
        copies[-1].start()
        mixed = mixed + jnp.dot(normed, value_ref[span, :], preferred_element_type=F32)
    value_half = (mixed * value_scale_ref[...]).astype(BF16)
    half_ref[...] = value_half
    squares = jnp.zeros((tokens, 128), F32)
    scores = jnp.zeros((tokens, 128), F32)
    for j in range(width // tile):
        span = slice(tile * j, tile * (j + 1))
        branch = lax.dot_general(
            value_half, out_ref[span, :], (((1,), (1,)), ((), ())), preferred_element_type=F32
        )
        residual = (hidden_ref[:, span].astype(F32) + branch * scale_ref[:, span]).astype(BF16)
        resid_ref[:, span] = residual
        copies.append(pltpu.make_async_copy(resid_ref.at[:, span], resid_out.at[:, span], sems.at[1, j]))
        copies[-1].start()
        resid32 = residual.astype(F32)
        squares = squares + lane_fold(resid32 * resid32)
        scores = scores + lane_fold(resid32 * weighted_ref[:, span])
    final_root = jnp.sqrt(jnp.sum(squares, axis=1, keepdims=True) / width + EPSILON)
    raw_score = jnp.sum(scores, axis=1, keepdims=True) / final_root
    capped = jnp.tanh(raw_score / SOFT_CAP)
    slope = 1.0 - capped * capped
    lead = slope / final_root
    pull = slope * raw_score / (width * final_root * final_root)
    lanes = lax.broadcasted_iota(jnp.int32, (tokens, 128), 1)
    columns_ref[...] = jnp.where(lanes == 0, lead, pull)
    member = segment_ref[...] == lanes
    sums = jnp.sum(jnp.where(member, SOFT_CAP * capped, 0.0), axis=0, keepdims=True)
    counts = jnp.sum(jnp.where(member, 1.0, 0.0), axis=0, keepdims=True)
    row = lax.broadcasted_iota(jnp.int32, (8, 128), 0)
    packed = jnp.where(row == 0, sums, counts)
    for k in range(stats_ref.shape[0]):
        stats_ref[k] = packed
    for copy in copies:
        copy.wait()


def backward_kernel(
    core_ref,
    resid_ref,
    own_ref,
    beside_ref,
    columns_ref,
    scale_ref,
    weighted_ref,
    value_scale_ref,
    unit_out,
    values_ref,
    out_ref,
    unit_ref,
    sems,
):
    tokens, width = resid_ref.shape
    rows = width // (own_ref.shape[0] * own_ref.shape[1])
    tile = 640

    @pl.when(core_ref[0] == 0)
    def _():
        place(beside_ref, rows, out_ref)

    @pl.when(core_ref[0] != 0)
    def _():
        place(own_ref, rows, out_ref)

    copies = []
    lead = columns_ref[:, 0:1]
    pull = columns_ref[:, 1:2]
    total = jnp.zeros(values_ref.shape, F32)
    for j in range(width // tile):
        span = slice(tile * j, tile * (j + 1))
        slope = lead * weighted_ref[:, span] - pull * resid_ref[:, span].astype(F32)
        unit = (slope * scale_ref[:, span]).astype(BF16)
        unit_ref[:, span] = unit
        copies.append(pltpu.make_async_copy(unit_ref.at[:, span], unit_out.at[:, span], sems.at[j]))
        copies[-1].start()
        total = total + jnp.dot(unit, out_ref[span, :], preferred_element_type=F32)
    values_ref[...] = total * value_scale_ref[...]
    for copy in copies:
        copy.wait()


def term_kernel(pick_ref, normed_ref, unit_ref, values_ref, half_ref, factor_ref, term_ref, small_ref):
    @pl.when(pl.program_id(0) == 0)
    def _():
        side = jnp.where(pick_ref[0] == 0, values_ref[...], half_ref[...].astype(F32))
        small_ref[...] = (factor_ref[...] * side).T.astype(BF16)

    def fill(tall_ref):
        term = jnp.dot(small_ref[...], tall_ref[...], preferred_element_type=F32)
        term_ref[...] = term.T.astype(term_ref.dtype)

    @pl.when(pick_ref[0] == 0)
    def _():
        fill(normed_ref)

    @pl.when(pick_ref[0] != 0)
    def _():
        fill(unit_ref)


def run_forward(core, hidden, root, own, beside, gain, scale, weighted, value_scale, segment):
    tokens, width = hidden.shape
    head = value_scale.shape[1]
    shape = jax.ShapeDtypeStruct
    vmem = pl.BlockSpec(memory_space=pltpu.VMEM)
    far = pl.BlockSpec(memory_space=pltpu.HBM)
    return pl.pallas_call(
        forward_kernel,
        out_shape=(
            shape((tokens, width), BF16),
            shape((tokens, width), BF16),
            shape((tokens, head), BF16),
            shape((tokens, 128), F32),
            shape((LIST_DEVICES, 8, 128), F32),
        ),
        in_specs=[pl.BlockSpec(memory_space=pltpu.SMEM)] + [vmem] * 9,
        out_specs=(far, far, vmem, vmem, vmem),
        scratch_shapes=[
            pltpu.VMEM((width, head), BF16),
            pltpu.VMEM((width, head), BF16),
            pltpu.VMEM((tokens, width), BF16),
            pltpu.VMEM((tokens, width), BF16),
            pltpu.SemaphoreType.DMA((2, width // 640)),
        ],
        compiler_params=pltpu.CompilerParams(vmem_limit_bytes=VMEM_LIMIT),
        cost_estimate=pl.CostEstimate(
            flops=4 * tokens * width * head, bytes_accessed=12 * width * tokens, transcendentals=tokens
        ),
        name="forward",
    )(core, hidden, root, own, beside, gain, scale, weighted, value_scale, segment)


def run_backward(core, resid, own, beside, columns, scale, weighted, value_scale):
    tokens, width = resid.shape
    head = value_scale.shape[1]
    vmem = pl.BlockSpec(memory_space=pltpu.VMEM)
    far = pl.BlockSpec(memory_space=pltpu.HBM)
    return pl.pallas_call(
        backward_kernel,
        out_shape=(
            jax.ShapeDtypeStruct((tokens, width), BF16),
            jax.ShapeDtypeStruct((tokens, head), F32),
        ),
        in_specs=[pl.BlockSpec(memory_space=pltpu.SMEM)] + [vmem] * 7,
        out_specs=(far, vmem),
        scratch_shapes=[
            pltpu.VMEM((width, head), BF16),
            pltpu.VMEM((tokens, width), BF16),
            pltpu.SemaphoreType.DMA((width // 640,)),
        ],
        compiler_params=pltpu.CompilerParams(vmem_limit_bytes=VMEM_LIMIT),
        cost_estimate=pl.CostEstimate(
            flops=2 * tokens * width * head, bytes_accessed=8 * width * tokens, transcendentals=0
        ),
        name="backward",
    )(core, resid, own, beside, columns, scale, weighted, value_scale)


def run_term(pick, normed, unit, values, half, factor, dtype):
    tokens, width = normed.shape
    head = values.shape[1]
    tile = width // 2
    whole = lambda j, pick: (0, 0)
    return pl.pallas_call(
        term_kernel,
        out_shape=jax.ShapeDtypeStruct((width, head), dtype),
        grid_spec=pltpu.PrefetchScalarGridSpec(
            num_scalar_prefetch=1,
            grid=(width // tile,),
            in_specs=[
                pl.BlockSpec((tokens, tile), lambda j, pick: (0, j * (1 - pick[0]))),
                pl.BlockSpec((tokens, tile), lambda j, pick: (0, j * pick[0])),
                pl.BlockSpec((tokens, head), whole),
                pl.BlockSpec((tokens, head), whole),
                pl.BlockSpec((tokens, 1), whole),
            ],
            out_specs=pl.BlockSpec((tile, head), lambda j, pick: (j, 0)),
            scratch_shapes=[pltpu.VMEM((head, tokens), BF16)],
        ),
        compiler_params=pltpu.CompilerParams(vmem_limit_bytes=TERM_LIMIT),
        cost_estimate=pl.CostEstimate(
            flops=2 * tokens * width * head, bytes_accessed=4 * width * tokens, transcendentals=0
        ),
        name="term",
    )(pick, normed, unit, values, half, factor)


def shards(
    hidden,
    segment,
    grades,
    value_codes,
    value_scale,
    output_codes,
    output_scale,
    norm_gain,
    final_gain,
    score_vector,
):
    rows, head_size = value_codes.shape
    core = lax.axis_index("c")
    first = core == 0
    tokens = hidden[0]
    width = tokens.shape[1]
    seg_local = segment[0][:, None]
    grade_rows = grades[0]
    cand_count = grade_rows.shape[1]

    with jax.named_scope("gather"):
        vectors = jnp.where(
            first, jnp.stack([norm_gain, output_scale]), jnp.stack([final_gain, score_vector])
        )
        vectors = jnp.pad(vectors, ((0, 6), (0, head_size - rows)))
        mine = jnp.concatenate([jnp.where(first, value_codes, output_codes), vectors], axis=0)
        other = lax.ppermute(mine, Z, half_partner())
        block = jnp.where(lax.axis_index("zh") == lax.axis_index("zb"), mine, other)
        column = lax.all_to_all(jnp.broadcast_to(block, (8,) + block.shape), Y, 0, 0)
        spread = jnp.broadcast_to(column, (8,) + column.shape)
        own = lax.all_to_all(spread, XB, 0, 0)
        tokens32 = tokens.astype(F32)
        root = jnp.sqrt(jnp.mean(tokens32 * tokens32, axis=-1, keepdims=True) + EPSILON)
        beside = lax.ppermute(own, "c", SWAP)

        def vector(block, which):
            parts = block[:, :, rows + which, :rows]
            return jnp.swapaxes(parts, 0, 1).reshape(1, width).astype(F32)

        gain32 = jnp.where(first, vector(own, 0), vector(beside, 0))
        scale32 = jnp.where(first, vector(own, 1), vector(beside, 1))
        final32 = jnp.where(first, vector(beside, 0), vector(own, 0))
        score32 = jnp.where(first, vector(beside, 1), vector(own, 1))
        weighted = final32 * score32

    value_row = value_scale[None, :]
    pick = core.astype(jnp.int32)[None]
    normed, resid, value_half, columns, stats = run_forward(
        pick, tokens, root, own, beside, gain32, scale32, weighted, value_row, seg_local
    )
    with jax.named_scope("stats"):
        arrived = lax.all_to_all(stats, ("yl", "x", "zh"), 0, 0)

    unit, values = run_backward(pick, resid, own, beside, columns, scale32, weighted, value_row)

    with jax.named_scope("factor"):
        stats = jnp.sum(arrived, axis=0)
        sums, counts = stats[0, :cand_count], stats[1, :cand_count]
        cand_score = sums / counts
        teacher = lax.dynamic_index_in_dim(grade_rows, lax.axis_index("yh"), 0, keepdims=False)
        teacher = teacher.astype(F32)
        log_teacher = teacher - jnp.log(jnp.sum(jnp.exp(teacher)))
        log_student = cand_score - jnp.log(jnp.sum(jnp.exp(cand_score)))
        own_loss = jnp.sum(jnp.exp(log_teacher) * (log_teacher - log_student))
        grad_cand = (jnp.exp(log_student) - jnp.exp(log_teacher)) / counts
        member = (seg_local == jnp.arange(cand_count, dtype=jnp.int32)).astype(F32)
        factor = jnp.sum(member * grad_cand, axis=-1, keepdims=True)

    give = run_term(1 - pick, normed, unit, values, value_half, factor, BF16)
    with jax.named_scope("reduce"):
        got = lax.ppermute(give, "c", SWAP)
        keep = run_term(pick, normed, unit, values, value_half, factor, F32)
        both = (keep + got.astype(F32)).astype(BF16)
        loss_hi = own_loss.astype(BF16)
        loss_lo = (own_loss - loss_hi.astype(F32)).astype(BF16)
        both, loss_hi, loss_lo = lax.optimization_barrier((both, loss_hi, loss_lo))
        loss_row = jnp.pad(jnp.stack([loss_hi, loss_lo])[None, :], ((0, 7), (0, head_size - 2)))
        half = rows // 2
        sent = both.reshape(8, 4, 2, 2, half, head_size).transpose(1, 3, 0, 2, 4, 5)
        came = lax.all_to_all(sent.reshape(8, 8 * rows, head_size), XB, 0, 0)
        part = jnp.sum(came.astype(F32), axis=0).astype(BF16).reshape(8, rows, head_size)
        part = jnp.concatenate([part, jnp.broadcast_to(loss_row, (8, 8, head_size))], axis=1)
        came = lax.all_to_all(part, Y, 0, 0)
        losses = came.reshape(4, 2, rows + 8, head_size)[:, 0, rows, :2]
        list_loss = jnp.sum(losses.astype(F32), axis=-1)
        part = jnp.sum(came[:, :rows].astype(F32), axis=0).astype(BF16)
        part, list_loss = lax.optimization_barrier((part, list_loss))
        part = part.reshape(2, 1, half, head_size)
        part = jnp.broadcast_to(part, (2, 6, half, head_size)).reshape(12, half, head_size)
        came = lax.all_to_all(part, Z, 0, 0).astype(F32)
        total = jnp.sum(came.reshape(6, 2, half, head_size), axis=0).reshape(rows, head_size)
        pair = lax.all_gather(total, "c")
    return (pair[0], pair[1], list_loss[None, :])


def solution(mesh):
    grid = Mesh(mesh.devices.reshape(4, 2, 4, 2, 3, 2, 2), WIDE + NARROW)
    in_specs = (
        P(NARROW, WIDE, None),
        P(NARROW, WIDE),
        P(NARROW, None, None),
        P(WIDE, None),
        P(),
        P(WIDE, None),
        P(WIDE),
        P(WIDE),
        P(WIDE),
        P(WIDE),
    )
    out_specs = (P(WIDE, None), P(WIDE, None), P(NARROW, None))
    return jax.shard_map(shards, mesh=grid, in_specs=in_specs, out_specs=out_specs, check_vma=False)
```

```python
import jax
import jax.numpy as jnp
from jax import lax
from jax.experimental import pallas as pl
from jax.experimental.pallas import tpu as pltpu
from jax.sharding import Mesh, PartitionSpec as P

EPSILON = 1e-06
SOFT_CAP = 30.0
Y = ("yh", "yl")
WIDE = ("yh", "yl", "x", "zh")
NARROW = ("za", "zb", "c")
Z = ("zh", "za", "zb")
XB = ("x", "zb")
SWAP = [(0, 1), (1, 0)]
LIST_DEVICES = 16
VMEM_LIMIT = 50 * 1024 * 1024
TERM_LIMIT = 52 * 1024 * 1024
F32 = jnp.float32
BF16 = jnp.bfloat16


def half_partner():
    pairs = []
    for z in range(12):
        if z // 6 != z % 2:
            pairs.append((z, (z + 3) % 12 if z % 6 >= 3 else (z - 3) % 12))
    return pairs


def place(source_ref, rows, target_ref):
    pairs, ys = source_ref.shape[0], source_ref.shape[1]
    for y in range(ys):
        for k in range(pairs):
            at = rows * (y * pairs + k)
            target_ref[at : at + rows, :] = source_ref[k, y, :rows, :]


def lane_fold(x):
    total = x[:, :128]
    for k in range(1, x.shape[1] // 128):
        total = total + x[:, 128 * k : 128 * (k + 1)]
    return total


def forward_kernel(
    core_ref,
    hidden_ref,
    root_ref,
    own_ref,
    beside_ref,
    gain_ref,
    scale_ref,
    weighted_ref,
    value_scale_ref,
    segment_ref,
    normed_out,
    resid_out,
    half_ref,
    columns_ref,
    stats_ref,
    value_ref,
    out_ref,
    normed_ref,
    resid_ref,
    sems,
):
    tokens, width = hidden_ref.shape
    rows = width // (own_ref.shape[0] * own_ref.shape[1])
    tile = 640

    @pl.when(core_ref[0] == 0)
    def _():
        place(own_ref, rows, value_ref)
        place(beside_ref, rows, out_ref)

    @pl.when(core_ref[0] != 0)
    def _():
        place(beside_ref, rows, value_ref)
        place(own_ref, rows, out_ref)

    copies = []
    inverse = 1.0 / root_ref[...]
    mixed = jnp.zeros((tokens, value_ref.shape[1]), F32)
    for j in range(width // tile):
        span = slice(tile * j, tile * (j + 1))
        scaled = hidden_ref[:, span].astype(F32) * inverse
        normed = (scaled * gain_ref[:, span]).astype(BF16)
        normed_ref[:, span] = normed
        copies.append(pltpu.make_async_copy(normed_ref.at[:, span], normed_out.at[:, span], sems.at[0, j]))
        copies[-1].start()
        mixed = mixed + jnp.dot(normed, value_ref[span, :], preferred_element_type=F32)
    value_half = (mixed * value_scale_ref[...]).astype(BF16)
    half_ref[...] = value_half
    squares = jnp.zeros((tokens, 128), F32)
    scores = jnp.zeros((tokens, 128), F32)
    for j in range(width // tile):
        span = slice(tile * j, tile * (j + 1))
        branch = lax.dot_general(
            value_half, out_ref[span, :], (((1,), (1,)), ((), ())), preferred_element_type=F32
        )
        residual = (hidden_ref[:, span].astype(F32) + branch * scale_ref[:, span]).astype(BF16)
        resid_ref[:, span] = residual
        copies.append(pltpu.make_async_copy(resid_ref.at[:, span], resid_out.at[:, span], sems.at[1, j]))
        copies[-1].start()
        resid32 = residual.astype(F32)
        squares = squares + lane_fold(resid32 * resid32)
        scores = scores + lane_fold(resid32 * weighted_ref[:, span])
    final_root = jnp.sqrt(jnp.sum(squares, axis=1, keepdims=True) / width + EPSILON)
    raw_score = jnp.sum(scores, axis=1, keepdims=True) / final_root
    capped = jnp.tanh(raw_score / SOFT_CAP)
    slope = 1.0 - capped * capped
    lead = slope / final_root
    pull = slope * raw_score / (width * final_root * final_root)
    lanes = lax.broadcasted_iota(jnp.int32, (tokens, 128), 1)
    columns_ref[...] = jnp.where(lanes == 0, lead, pull)
    member = segment_ref[...] == lanes
    sums = jnp.sum(jnp.where(member, SOFT_CAP * capped, 0.0), axis=0, keepdims=True)
    counts = jnp.sum(jnp.where(member, 1.0, 0.0), axis=0, keepdims=True)
    row = lax.broadcasted_iota(jnp.int32, (8, 128), 0)
    packed = jnp.where(row == 0, sums, counts)
    for k in range(stats_ref.shape[0]):
        stats_ref[k] = packed
    for copy in copies:
        copy.wait()


def backward_kernel(
    core_ref,
    resid_ref,
    own_ref,
    beside_ref,
    columns_ref,
    scale_ref,
    weighted_ref,
    value_scale_ref,
    unit_ref,
    values_ref,
    out_ref,
):
    tokens, width = resid_ref.shape
    rows = width // (own_ref.shape[0] * own_ref.shape[1])
    tile = 640

    @pl.when(core_ref[0] == 0)
    def _():
        place(beside_ref, rows, out_ref)

    @pl.when(core_ref[0] != 0)
    def _():
        place(own_ref, rows, out_ref)

    lead = columns_ref[:, 0:1]
    pull = columns_ref[:, 1:2]
    total = jnp.zeros(values_ref.shape, F32)
    for j in range(width // tile):
        span = slice(tile * j, tile * (j + 1))
        slope = lead * weighted_ref[:, span] - pull * resid_ref[:, span].astype(F32)
        unit = (slope * scale_ref[:, span]).astype(BF16)
        unit_ref[:, span] = unit
        total = total + jnp.dot(unit, out_ref[span, :], preferred_element_type=F32)
    values_ref[...] = total * value_scale_ref[...]


def term_kernel(pick_ref, normed_ref, unit_ref, values_ref, half_ref, factor_ref, term_ref, small_ref):
    @pl.when(pl.program_id(0) == 0)
    def _():
        side = jnp.where(pick_ref[0] == 0, values_ref[...], half_ref[...].astype(F32))
        small_ref[...] = (factor_ref[...] * side).T.astype(BF16)

    def fill(tall_ref):
        term = jnp.dot(small_ref[...], tall_ref[...], preferred_element_type=F32)
        term_ref[...] = term.T.astype(term_ref.dtype)

    @pl.when(pick_ref[0] == 0)
    def _():
        fill(normed_ref)

    @pl.when(pick_ref[0] != 0)
    def _():
        fill(unit_ref)


def run_forward(core, hidden, root, own, beside, gain, scale, weighted, value_scale, segment):
    tokens, width = hidden.shape
    head = value_scale.shape[1]
    shape = jax.ShapeDtypeStruct
    vmem = pl.BlockSpec(memory_space=pltpu.VMEM)
    far = pl.BlockSpec(memory_space=pltpu.HBM)
    return pl.pallas_call(
        forward_kernel,
        out_shape=(
            shape((tokens, width), BF16),
            shape((tokens, width), BF16),
            shape((tokens, head), BF16),
            shape((tokens, 128), F32),
            shape((LIST_DEVICES, 8, 128), F32),
        ),
        in_specs=[pl.BlockSpec(memory_space=pltpu.SMEM)] + [vmem] * 9,
        out_specs=(far, far, vmem, vmem, vmem),
        scratch_shapes=[
            pltpu.VMEM((width, head), BF16),
            pltpu.VMEM((width, head), BF16),
            pltpu.VMEM((tokens, width), BF16),
            pltpu.VMEM((tokens, width), BF16),
            pltpu.SemaphoreType.DMA((2, width // 640)),
        ],
        compiler_params=pltpu.CompilerParams(vmem_limit_bytes=VMEM_LIMIT),
        cost_estimate=pl.CostEstimate(
            flops=4 * tokens * width * head, bytes_accessed=12 * width * tokens, transcendentals=tokens
        ),
        name="forward",
    )(core, hidden, root, own, beside, gain, scale, weighted, value_scale, segment)


def run_backward(core, resid, own, beside, columns, scale, weighted, value_scale):
    tokens, width = resid.shape
    head = value_scale.shape[1]
    vmem = pl.BlockSpec(memory_space=pltpu.VMEM)
    return pl.pallas_call(
        backward_kernel,
        out_shape=(
            jax.ShapeDtypeStruct((tokens, width), BF16),
            jax.ShapeDtypeStruct((tokens, head), F32),
        ),
        in_specs=[pl.BlockSpec(memory_space=pltpu.SMEM)] + [vmem] * 7,
        out_specs=(vmem,) * 2,
        scratch_shapes=[pltpu.VMEM((width, head), BF16)],
        compiler_params=pltpu.CompilerParams(vmem_limit_bytes=VMEM_LIMIT),
        cost_estimate=pl.CostEstimate(
            flops=2 * tokens * width * head, bytes_accessed=8 * width * tokens, transcendentals=0
        ),
        name="backward",
    )(core, resid, own, beside, columns, scale, weighted, value_scale)


def run_term(pick, normed, unit, values, half, factor, dtype):
    tokens, width = normed.shape
    head = values.shape[1]
    tile = width // 2
    whole = lambda j, pick: (0, 0)
    return pl.pallas_call(
        term_kernel,
        out_shape=jax.ShapeDtypeStruct((width, head), dtype),
        grid_spec=pltpu.PrefetchScalarGridSpec(
            num_scalar_prefetch=1,
            grid=(width // tile,),
            in_specs=[
                pl.BlockSpec((tokens, tile), lambda j, pick: (0, j * (1 - pick[0]))),
                pl.BlockSpec((tokens, tile), lambda j, pick: (0, j * pick[0])),
                pl.BlockSpec((tokens, head), whole),
                pl.BlockSpec((tokens, head), whole),
                pl.BlockSpec((tokens, 1), whole),
            ],
            out_specs=pl.BlockSpec((tile, head), lambda j, pick: (j, 0)),
            scratch_shapes=[pltpu.VMEM((head, tokens), BF16)],
        ),
        compiler_params=pltpu.CompilerParams(vmem_limit_bytes=TERM_LIMIT),
        cost_estimate=pl.CostEstimate(
            flops=2 * tokens * width * head, bytes_accessed=4 * width * tokens, transcendentals=0
        ),
        name="term",
    )(pick, normed, unit, values, half, factor)


def shards(
    hidden,
    segment,
    grades,
    value_codes,
    value_scale,
    output_codes,
    output_scale,
    norm_gain,
    final_gain,
    score_vector,
):
    rows, head_size = value_codes.shape
    core = lax.axis_index("c")
    first = core == 0
    tokens = hidden[0]
    width = tokens.shape[1]
    seg_local = segment[0][:, None]
    grade_rows = grades[0]
    cand_count = grade_rows.shape[1]

    with jax.named_scope("gather"):
        vectors = jnp.where(
            first, jnp.stack([norm_gain, output_scale]), jnp.stack([final_gain, score_vector])
        )
        vectors = jnp.pad(vectors, ((0, 6), (0, head_size - rows)))
        mine = jnp.concatenate([jnp.where(first, value_codes, output_codes), vectors], axis=0)
        other = lax.ppermute(mine, Z, half_partner())
        block = jnp.where(lax.axis_index("zh") == lax.axis_index("zb"), mine, other)
        column = lax.all_to_all(jnp.broadcast_to(block, (8,) + block.shape), Y, 0, 0)
        spread = jnp.broadcast_to(column, (8,) + column.shape)
        own = lax.all_to_all(spread, XB, 0, 0)
        tokens32 = tokens.astype(F32)
        root = jnp.sqrt(jnp.mean(tokens32 * tokens32, axis=-1, keepdims=True) + EPSILON)
        beside = lax.ppermute(own, "c", SWAP)

        def vector(block, which):
            parts = block[:, :, rows + which, :rows]
            return jnp.swapaxes(parts, 0, 1).reshape(1, width).astype(F32)

        gain32 = jnp.where(first, vector(own, 0), vector(beside, 0))
        scale32 = jnp.where(first, vector(own, 1), vector(beside, 1))
        final32 = jnp.where(first, vector(beside, 0), vector(own, 0))
        score32 = jnp.where(first, vector(beside, 1), vector(own, 1))
        weighted = final32 * score32

    value_row = value_scale[None, :]
    pick = core.astype(jnp.int32)[None]
    normed, resid, value_half, columns, stats = run_forward(
        pick, tokens, root, own, beside, gain32, scale32, weighted, value_row, seg_local
    )
    with jax.named_scope("stats"):
        arrived = lax.all_to_all(stats, ("yl", "x", "zh"), 0, 0)

    unit, values = run_backward(pick, resid, own, beside, columns, scale32, weighted, value_row)

    with jax.named_scope("factor"):
        stats = jnp.sum(arrived, axis=0)
        sums, counts = stats[0, :cand_count], stats[1, :cand_count]
        cand_score = sums / counts
        teacher = lax.dynamic_index_in_dim(grade_rows, lax.axis_index("yh"), 0, keepdims=False)
        teacher = teacher.astype(F32)
        log_teacher = teacher - jnp.log(jnp.sum(jnp.exp(teacher)))
        log_student = cand_score - jnp.log(jnp.sum(jnp.exp(cand_score)))
        own_loss = jnp.sum(jnp.exp(log_teacher) * (log_teacher - log_student))
        grad_cand = (jnp.exp(log_student) - jnp.exp(log_teacher)) / counts
        member = (seg_local == jnp.arange(cand_count, dtype=jnp.int32)).astype(F32)
        factor = jnp.sum(member * grad_cand, axis=-1, keepdims=True)

    give = run_term(1 - pick, normed, unit, values, value_half, factor, BF16)
    with jax.named_scope("reduce"):
        got = lax.ppermute(give, "c", SWAP)
        keep = run_term(pick, normed, unit, values, value_half, factor, F32)
        both = (keep + got.astype(F32)).astype(BF16)
        loss_hi = own_loss.astype(BF16)
        loss_lo = (own_loss - loss_hi.astype(F32)).astype(BF16)
        loss_row = jnp.pad(jnp.stack([loss_hi, loss_lo])[None, :], ((0, 7), (0, head_size - 2)))
        both, loss_row = lax.optimization_barrier((both, jnp.broadcast_to(loss_row, (8, 8, head_size))))
        half = rows // 2
        sent = both.reshape(8, 4, 2, 2, half, head_size).transpose(1, 3, 0, 2, 4, 5)
        came = lax.all_to_all(sent.reshape(8, 8 * rows, head_size), XB, 0, 0)
        part = jnp.sum(came.astype(F32), axis=0).astype(BF16).reshape(8, rows, head_size)
        part = jnp.concatenate([part, loss_row], axis=1)
        came = lax.all_to_all(part, Y, 0, 0)
        losses = came.reshape(4, 2, rows + 8, head_size)[:, 0, rows, :2]
        list_loss = jnp.sum(losses.astype(F32), axis=-1)
        part = jnp.sum(came[:, :rows].astype(F32), axis=0).astype(BF16)
        part, list_loss = lax.optimization_barrier((part, list_loss))
        part = part.reshape(2, 1, half, head_size)
        part = jnp.broadcast_to(part, (2, 6, half, head_size)).reshape(12, half, head_size)
        came = lax.all_to_all(part, Z, 0, 0).astype(F32)
        total = jnp.sum(came.reshape(6, 2, half, head_size), axis=0).reshape(rows, head_size)
        pair = lax.all_gather(total, "c")
    return (pair[0], pair[1], list_loss[None, :])


def solution(mesh):
    grid = Mesh(mesh.devices.reshape(4, 2, 4, 2, 3, 2, 2), WIDE + NARROW)
    in_specs = (
        P(NARROW, WIDE, None),
        P(NARROW, WIDE),
        P(NARROW, None, None),
        P(WIDE, None),
        P(),
        P(WIDE, None),
        P(WIDE),
        P(WIDE),
        P(WIDE),
        P(WIDE),
    )
    out_specs = (P(WIDE, None), P(WIDE, None), P(NARROW, None))
    return jax.shard_map(shards, mesh=grid, in_specs=in_specs, out_specs=out_specs, check_vma=False)
```

```python
import jax
import jax.numpy as jnp
from jax import lax
from jax.experimental import pallas as pl
from jax.experimental.pallas import tpu as pltpu
from jax.sharding import Mesh, PartitionSpec as P

EPSILON = 1e-06
SOFT_CAP = 30.0
Y = ("yh", "yl")
WIDE = ("yh", "yl", "x", "zh")
NARROW = ("za", "zb", "c")
Z = ("zh", "za", "zb")
XB = ("x", "zb")
SWAP = [(0, 1), (1, 0)]
LIST_DEVICES = 16
CANDS = 20
VMEM_LIMIT = 50 * 1024 * 1024
TERM_LIMIT = 52 * 1024 * 1024
F32 = jnp.float32
BF16 = jnp.bfloat16


def half_partner():
    pairs = []
    for z in range(12):
        if z // 6 != z % 2:
            pairs.append((z, (z + 3) % 12 if z % 6 >= 3 else (z - 3) % 12))
    return pairs


def place(source_ref, rows, target_ref):
    pairs = source_ref.shape[0]
    for y in range(target_ref.shape[0] // (rows * pairs)):
        for k in range(pairs):
            at = rows * (y * pairs + k)
            target_ref[at : at + rows, :] = source_ref[k, rows * y : rows * (y + 1), :]


def lane_fold(x):
    total = x[:, :128]
    for k in range(1, x.shape[1] // 128):
        total = total + x[:, 128 * k : 128 * (k + 1)]
    return total


def forward_kernel(
    core_ref,
    hidden_in,
    root_ref,
    own_ref,
    beside_ref,
    gain_ref,
    scale_ref,
    weighted_ref,
    value_scale_ref,
    segment_ref,
    normed_out,
    resid_out,
    half_ref,
    columns_ref,
    stats_ref,
    value_ref,
    out_ref,
    normed_ref,
    resid_ref,
    hidden_ref,
    sems,
):
    tokens, width = hidden_ref.shape
    rows = width // 64
    tile = 640
    loads = []
    for j in range(width // tile):
        span = slice(tile * j, tile * (j + 1))
        loads.append(pltpu.make_async_copy(hidden_in.at[:, span], hidden_ref.at[:, span], sems.at[2, j]))
        loads[-1].start()

    @pl.when(core_ref[0] == 0)
    def _():
        place(own_ref, rows, value_ref)
        place(beside_ref, rows, out_ref)

    @pl.when(core_ref[0] != 0)
    def _():
        place(beside_ref, rows, value_ref)
        place(own_ref, rows, out_ref)

    copies = []
    inverse = 1.0 / root_ref[...]
    mixed = jnp.zeros((tokens, value_ref.shape[1]), F32)
    for j in range(width // tile):
        span = slice(tile * j, tile * (j + 1))
        loads[j].wait()
        scaled = hidden_ref[:, span].astype(F32) * inverse
        normed = (scaled * gain_ref[:, span]).astype(BF16)
        normed_ref[:, span] = normed
        copies.append(pltpu.make_async_copy(normed_ref.at[:, span], normed_out.at[:, span], sems.at[0, j]))
        copies[-1].start()
        mixed = mixed + jnp.dot(normed, value_ref[span, :], preferred_element_type=F32)
    value_half = (mixed * value_scale_ref[...]).astype(BF16)
    half_ref[...] = value_half
    squares = jnp.zeros((tokens, 128), F32)
    scores = jnp.zeros((tokens, 128), F32)
    for j in range(width // tile):
        span = slice(tile * j, tile * (j + 1))
        branch = lax.dot_general(
            value_half, out_ref[span, :], (((1,), (1,)), ((), ())), preferred_element_type=F32
        )
        residual = (hidden_ref[:, span].astype(F32) + branch * scale_ref[:, span]).astype(BF16)
        resid_ref[:, span] = residual
        copies.append(pltpu.make_async_copy(resid_ref.at[:, span], resid_out.at[:, span], sems.at[1, j]))
        copies[-1].start()
        resid32 = residual.astype(F32)
        squares = squares + lane_fold(resid32 * resid32)
        scores = scores + lane_fold(resid32 * weighted_ref[:, span])
    final_root = jnp.sqrt(jnp.sum(squares, axis=1, keepdims=True) / width + EPSILON)
    raw_score = jnp.sum(scores, axis=1, keepdims=True) / final_root
    capped = jnp.tanh(raw_score / SOFT_CAP)
    slope = 1.0 - capped * capped
    lead = slope / final_root
    pull = slope * raw_score / (width * final_root * final_root)
    lanes = lax.broadcasted_iota(jnp.int32, (tokens, 128), 1)
    columns_ref[...] = jnp.where(lanes == 0, lead, pull)
    member = segment_ref[...] == lanes
    sums = jnp.sum(jnp.where(member, SOFT_CAP * capped, 0.0), axis=0, keepdims=True)
    counts = jnp.sum(jnp.where(member, 1.0, 0.0), axis=0, keepdims=True)
    row = lax.broadcasted_iota(jnp.int32, (8, 128), 0)
    packed = jnp.where(row == 0, sums, counts)
    for k in range(stats_ref.shape[0]):
        stats_ref[k] = packed
    for copy in copies:
        copy.wait()


def backward_kernel(
    core_ref,
    resid_ref,
    own_ref,
    beside_ref,
    columns_ref,
    scale_ref,
    weighted_ref,
    value_scale_ref,
    unit_ref,
    values_ref,
    out_ref,
):
    tokens, width = resid_ref.shape
    rows = width // 64
    tile = 640

    @pl.when(core_ref[0] == 0)
    def _():
        place(beside_ref, rows, out_ref)

    @pl.when(core_ref[0] != 0)
    def _():
        place(own_ref, rows, out_ref)

    lead = columns_ref[:, 0:1]
    pull = columns_ref[:, 1:2]
    total = jnp.zeros(values_ref.shape, F32)
    for j in range(width // tile):
        span = slice(tile * j, tile * (j + 1))
        slope = lead * weighted_ref[:, span] - pull * resid_ref[:, span].astype(F32)
        unit = (slope * scale_ref[:, span]).astype(BF16)
        unit_ref[:, span] = unit
        total = total + jnp.dot(unit, out_ref[span, :], preferred_element_type=F32)
    values_ref[...] = total * value_scale_ref[...]


def list_factor(arrived_ref, teacher_ref, segment_ref):
    stats = jnp.sum(arrived_ref[...], axis=0)
    lanes = lax.broadcasted_iota(jnp.int32, (1, 128), 1)
    real = lanes < CANDS
    counts = jnp.where(real, stats[1:2, :], 1.0)
    cand_score = jnp.where(real, stats[0:1, :] / counts, 0.0)
    teacher = teacher_ref[...]
    exp_teacher = jnp.where(real, jnp.exp(teacher), 0.0)
    exp_student = jnp.where(real, jnp.exp(cand_score), 0.0)
    log_teacher = teacher - jnp.log(jnp.sum(exp_teacher, axis=1, keepdims=True))
    log_student = cand_score - jnp.log(jnp.sum(exp_student, axis=1, keepdims=True))
    grad_cand = (jnp.exp(log_student) - jnp.exp(log_teacher)) / counts
    places = lax.broadcasted_iota(jnp.int32, (segment_ref.shape[0], 128), 1)
    member = segment_ref[...] == places
    return jnp.sum(jnp.where(member, grad_cand, 0.0), axis=1, keepdims=True)


def term_kernel(
    pick_ref,
    normed_ref,
    unit_ref,
    values_ref,
    half_ref,
    arrived_ref,
    teacher_ref,
    segment_ref,
    term_ref,
    small_ref,
):
    @pl.when(pl.program_id(0) == 0)
    def _():
        factor = list_factor(arrived_ref, teacher_ref, segment_ref)
        side = jnp.where(pick_ref[0] == 0, values_ref[...], half_ref[...].astype(F32))
        small_ref[...] = (factor * side).T.astype(BF16)

    def fill(tall_ref):
        term = jnp.dot(small_ref[...], tall_ref[...], preferred_element_type=F32)
        term_ref[...] = term.T.astype(term_ref.dtype)

    @pl.when(pick_ref[0] == 0)
    def _():
        fill(normed_ref)

    @pl.when(pick_ref[0] != 0)
    def _():
        fill(unit_ref)


def run_forward(core, hidden, root, own, beside, gain, scale, weighted, value_scale, segment):
    tokens, width = hidden.shape
    head = value_scale.shape[1]
    shape = jax.ShapeDtypeStruct
    vmem = pl.BlockSpec(memory_space=pltpu.VMEM)
    far = pl.BlockSpec(memory_space=pltpu.HBM)
    return pl.pallas_call(
        forward_kernel,
        out_shape=(
            shape((tokens, width), BF16),
            shape((tokens, width), BF16),
            shape((tokens, head), BF16),
            shape((tokens, 128), F32),
            shape((LIST_DEVICES, 8, 128), F32),
        ),
        in_specs=[pl.BlockSpec(memory_space=pltpu.SMEM), far] + [vmem] * 8,
        out_specs=(far, far, vmem, vmem, vmem),
        scratch_shapes=[
            pltpu.VMEM((width, head), BF16),
            pltpu.VMEM((width, head), BF16),
            pltpu.VMEM((tokens, width), BF16),
            pltpu.VMEM((tokens, width), BF16),
            pltpu.VMEM((tokens, width), BF16),
            pltpu.SemaphoreType.DMA((3, width // 640)),
        ],
        compiler_params=pltpu.CompilerParams(vmem_limit_bytes=VMEM_LIMIT),
        cost_estimate=pl.CostEstimate(
            flops=4 * tokens * width * head, bytes_accessed=12 * width * tokens, transcendentals=tokens
        ),
        name="forward",
    )(core, hidden, root, own, beside, gain, scale, weighted, value_scale, segment)


def run_backward(core, resid, own, beside, columns, scale, weighted, value_scale):
    tokens, width = resid.shape
    head = value_scale.shape[1]
    vmem = pl.BlockSpec(memory_space=pltpu.VMEM)
    return pl.pallas_call(
        backward_kernel,
        out_shape=(
            jax.ShapeDtypeStruct((tokens, width), BF16),
            jax.ShapeDtypeStruct((tokens, head), F32),
        ),
        in_specs=[pl.BlockSpec(memory_space=pltpu.SMEM)] + [vmem] * 7,
        out_specs=(vmem,) * 2,
        scratch_shapes=[pltpu.VMEM((width, head), BF16)],
        compiler_params=pltpu.CompilerParams(vmem_limit_bytes=VMEM_LIMIT),
        cost_estimate=pl.CostEstimate(
            flops=2 * tokens * width * head, bytes_accessed=8 * width * tokens, transcendentals=0
        ),
        name="backward",
    )(core, resid, own, beside, columns, scale, weighted, value_scale)


def run_term(pick, normed, unit, values, half, arrived, teacher, segment):
    tokens, width = normed.shape
    head = values.shape[1]
    tile = width // 2
    whole = lambda j, pick: (0, 0)
    return pl.pallas_call(
        term_kernel,
        out_shape=jax.ShapeDtypeStruct((width, head), BF16),
        grid_spec=pltpu.PrefetchScalarGridSpec(
            num_scalar_prefetch=1,
            grid=(width // tile,),
            in_specs=[
                pl.BlockSpec((tokens, tile), lambda j, pick: (0, j * (1 - pick[0]))),
                pl.BlockSpec((tokens, tile), lambda j, pick: (0, j * pick[0])),
                pl.BlockSpec((tokens, head), whole),
                pl.BlockSpec((tokens, head), whole),
                pl.BlockSpec(arrived.shape, lambda j, pick: (0, 0, 0)),
                pl.BlockSpec((1, 128), whole),
                pl.BlockSpec((tokens, 1), whole),
            ],
            out_specs=pl.BlockSpec((tile, head), lambda j, pick: (j, 0)),
            scratch_shapes=[pltpu.VMEM((head, tokens), BF16)],
        ),
        compiler_params=pltpu.CompilerParams(vmem_limit_bytes=TERM_LIMIT),
        cost_estimate=pl.CostEstimate(
            flops=2 * tokens * width * head, bytes_accessed=4 * width * tokens, transcendentals=0
        ),
        name="term",
    )(pick, normed, unit, values, half, arrived, teacher, segment)


def shards(
    hidden,
    segment,
    grades,
    value_codes,
    value_scale,
    output_codes,
    output_scale,
    norm_gain,
    final_gain,
    score_vector,
):
    rows, head_size = value_codes.shape
    core = lax.axis_index("c")
    first = core == 0
    tokens = hidden[0]
    width = tokens.shape[1]
    seg_local = segment[0][:, None]

    with jax.named_scope("gather"):
        vectors = jnp.where(
            first, jnp.stack([norm_gain, output_scale]), jnp.stack([final_gain, score_vector])
        )
        vectors = jnp.pad(vectors, ((0, 6), (0, head_size - rows)))
        mine = jnp.concatenate([jnp.where(first, value_codes, output_codes), vectors], axis=0)
        other = lax.ppermute(mine, Z, half_partner())
        block = jnp.where(lax.axis_index("zh") == lax.axis_index("zb"), mine, other)
        column = lax.all_to_all(jnp.broadcast_to(block, (8,) + block.shape), Y, 0, 0)
        column = jnp.concatenate(
            [
                column[:, :rows].reshape(8 * rows, head_size),
                column[:, rows : rows + 2].reshape(16, head_size),
            ],
            axis=0,
        )
        spread = jnp.broadcast_to(column, (8,) + column.shape)
        own = lax.all_to_all(spread, XB, 0, 0)
        tokens32 = tokens.astype(F32)
        root = jnp.sqrt(jnp.mean(tokens32 * tokens32, axis=-1, keepdims=True) + EPSILON)
        beside = lax.ppermute(own, "c", SWAP)

        def vector(block, which):
            parts = block[:, 8 * rows :, :rows].reshape(8, 8, 2, rows)[:, :, which]
            return jnp.swapaxes(parts, 0, 1).reshape(1, width).astype(F32)

        gain32 = jnp.where(first, vector(own, 0), vector(beside, 0))
        scale32 = jnp.where(first, vector(own, 1), vector(beside, 1))
        final32 = jnp.where(first, vector(beside, 0), vector(own, 0))
        score32 = jnp.where(first, vector(beside, 1), vector(own, 1))
        weighted = final32 * score32

    value_row = value_scale[None, :]
    pick = core.astype(jnp.int32)[None]
    normed, resid, value_half, columns, stats = run_forward(
        pick, tokens, root, own, beside, gain32, scale32, weighted, value_row, seg_local
    )
    with jax.named_scope("stats"):
        arrived = lax.all_to_all(stats, ("yl", "x", "zh"), 0, 0)

    unit, values = run_backward(pick, resid, own, beside, columns, scale32, weighted, value_row)

    teacher = lax.dynamic_index_in_dim(grades[0], lax.axis_index("yh"), 0, keepdims=True)
    teacher = jnp.pad(teacher.astype(F32), ((0, 0), (0, head_size - CANDS)))

    give = run_term(1 - pick, normed, unit, values, value_half, arrived, teacher, seg_local)
    with jax.named_scope("reduce"):
        got = lax.ppermute(give, "c", SWAP)
        keep = run_term(pick, normed, unit, values, value_half, arrived, teacher, seg_local)
        both = (keep.astype(F32) + got.astype(F32)).astype(BF16)
        stats = jnp.sum(arrived, axis=0)
        cand_score = stats[0, :CANDS] / stats[1, :CANDS]
        grade = teacher[0, :CANDS]
        log_teacher = grade - jnp.log(jnp.sum(jnp.exp(grade)))
        log_student = cand_score - jnp.log(jnp.sum(jnp.exp(cand_score)))
        own_loss = jnp.sum(jnp.exp(log_teacher) * (log_teacher - log_student))
        loss_hi = own_loss.astype(BF16)
        loss_lo = (own_loss - loss_hi.astype(F32)).astype(BF16)
        loss_row = jnp.pad(jnp.stack([loss_hi, loss_lo])[None, :], ((0, 7), (0, head_size - 2)))
        both, loss_row = lax.optimization_barrier((both, jnp.broadcast_to(loss_row, (8, 8, head_size))))
        half = rows // 2
        sent = both.reshape(8, 4, 2, 2, half, head_size).transpose(1, 3, 0, 2, 4, 5)
        came = lax.all_to_all(sent.reshape(8, 8 * rows, head_size), XB, 0, 0)
        part = jnp.sum(came.astype(F32), axis=0).astype(BF16).reshape(8, rows, head_size)
        part = jnp.concatenate([part, loss_row], axis=1)
        came = lax.all_to_all(part, Y, 0, 0)
        losses = came.reshape(4, 2, rows + 8, head_size)[:, 0, rows, :2]
        list_loss = jnp.sum(losses.astype(F32), axis=-1)
        part = jnp.sum(came[:, :rows].astype(F32), axis=0).astype(BF16)
        part, list_loss = lax.optimization_barrier((part, list_loss))
        part = part.reshape(2, 1, half, head_size)
        part = jnp.broadcast_to(part, (2, 6, half, head_size)).reshape(12, half, head_size)
        came = lax.all_to_all(part, Z, 0, 0).astype(F32)
        total = jnp.sum(came.reshape(6, 2, half, head_size), axis=0).reshape(rows, head_size)
        pair = lax.all_gather(total, "c")
    return (pair[0], pair[1], list_loss[None, :])


def solution(mesh):
    grid = Mesh(mesh.devices.reshape(4, 2, 4, 2, 3, 2, 2), WIDE + NARROW)
    in_specs = (
        P(NARROW, WIDE, None),
        P(NARROW, WIDE),
        P(NARROW, None, None),
        P(WIDE, None),
        P(),
        P(WIDE, None),
        P(WIDE),
        P(WIDE),
        P(WIDE),
        P(WIDE),
    )
    out_specs = (P(WIDE, None), P(WIDE, None), P(NARROW, None))
    return jax.shard_map(shards, mesh=grid, in_specs=in_specs, out_specs=out_specs, check_vma=False)
```

```python
import jax
import jax.numpy as jnp
from jax import lax
from jax.experimental import pallas as pl
from jax.experimental.pallas import tpu as pltpu
from jax.sharding import Mesh, PartitionSpec as P

EPSILON = 1e-06
SOFT_CAP = 30.0
Y = ("yh", "yl")
WIDE = ("yh", "yl", "x", "zh")
NARROW = ("za", "zb", "c")
Z = ("zh", "za", "zb")
XB = ("x", "zb")
SWAP = [(0, 1), (1, 0)]
LIST_DEVICES = 16
CANDS = 20
VMEM_LIMIT = 50 * 1024 * 1024
TERM_LIMIT = 52 * 1024 * 1024
F32 = jnp.float32
BF16 = jnp.bfloat16


def half_partner():
    pairs = []
    for z in range(12):
        if z // 6 != z % 2:
            pairs.append((z, (z + 3) % 12 if z % 6 >= 3 else (z - 3) % 12))
    return pairs


def place(source_ref, rows, target_ref):
    pairs = source_ref.shape[0]
    for y in range(target_ref.shape[0] // (rows * pairs)):
        for k in range(pairs):
            at = rows * (y * pairs + k)
            target_ref[at : at + rows, :] = source_ref[k, rows * y : rows * (y + 1), :]


def lane_fold(x):
    total = x[:, :128]
    for k in range(1, x.shape[1] // 128):
        total = total + x[:, 128 * k : 128 * (k + 1)]
    return total


def forward_kernel(
    core_ref,
    hidden_in,
    root_ref,
    own_ref,
    beside_ref,
    gain_ref,
    scale_ref,
    weighted_ref,
    value_scale_ref,
    segment_ref,
    normed_out,
    resid_out,
    half_ref,
    columns_ref,
    stats_ref,
    value_ref,
    out_ref,
    normed_ref,
    resid_ref,
    hidden_ref,
    sems,
):
    tokens, width = hidden_ref.shape
    rows = width // 64
    tile = 640
    loads = []
    for j in range(width // tile):
        span = slice(tile * j, tile * (j + 1))
        loads.append(pltpu.make_async_copy(hidden_in.at[:, span], hidden_ref.at[:, span], sems.at[2, j]))
        loads[-1].start()

    @pl.when(core_ref[0] == 0)
    def _():
        place(own_ref, rows, value_ref)
        place(beside_ref, rows, out_ref)

    @pl.when(core_ref[0] != 0)
    def _():
        place(beside_ref, rows, value_ref)
        place(own_ref, rows, out_ref)

    copies = []
    inverse = 1.0 / root_ref[...]
    mixed = jnp.zeros((tokens, value_ref.shape[1]), F32)
    for j in range(width // tile):
        span = slice(tile * j, tile * (j + 1))
        loads[j].wait()
        scaled = hidden_ref[:, span].astype(F32) * inverse
        normed = (scaled * gain_ref[:, span]).astype(BF16)
        normed_ref[:, span] = normed
        copies.append(pltpu.make_async_copy(normed_ref.at[:, span], normed_out.at[:, span], sems.at[0, j]))
        copies[-1].start()
        mixed = mixed + jnp.dot(normed, value_ref[span, :], preferred_element_type=F32)
    value_half = (mixed * value_scale_ref[...]).astype(BF16)
    half_ref[...] = value_half
    squares = jnp.zeros((tokens, 128), F32)
    scores = jnp.zeros((tokens, 128), F32)
    for j in range(width // tile):
        span = slice(tile * j, tile * (j + 1))
        branch = lax.dot_general(
            value_half, out_ref[span, :], (((1,), (1,)), ((), ())), preferred_element_type=F32
        )
        residual = (hidden_ref[:, span].astype(F32) + branch * scale_ref[:, span]).astype(BF16)
        resid_ref[:, span] = residual
        copies.append(pltpu.make_async_copy(resid_ref.at[:, span], resid_out.at[:, span], sems.at[1, j]))
        copies[-1].start()
        resid32 = residual.astype(F32)
        squares = squares + lane_fold(resid32 * resid32)
        scores = scores + lane_fold(resid32 * weighted_ref[:, span])
    final_root = jnp.sqrt(jnp.sum(squares, axis=1, keepdims=True) / width + EPSILON)
    raw_score = jnp.sum(scores, axis=1, keepdims=True) / final_root
    capped = jnp.tanh(raw_score / SOFT_CAP)
    slope = 1.0 - capped * capped
    lead = slope / final_root
    pull = slope * raw_score / (width * final_root * final_root)
    lanes = lax.broadcasted_iota(jnp.int32, (tokens, 128), 1)
    columns_ref[...] = jnp.where(lanes == 0, lead, pull)
    member = segment_ref[...] == lanes
    sums = jnp.sum(jnp.where(member, SOFT_CAP * capped, 0.0), axis=0, keepdims=True)
    counts = jnp.sum(jnp.where(member, 1.0, 0.0), axis=0, keepdims=True)
    row = lax.broadcasted_iota(jnp.int32, (8, 128), 0)
    packed = jnp.where(row == 0, sums, counts)
    for k in range(stats_ref.shape[0]):
        stats_ref[k] = packed
    for copy in copies:
        copy.wait()


def backward_kernel(
    core_ref,
    resid_ref,
    own_ref,
    beside_ref,
    columns_ref,
    scale_ref,
    weighted_ref,
    value_scale_ref,
    unit_ref,
    values_ref,
    out_ref,
):
    tokens, width = resid_ref.shape
    rows = width // 64
    tile = 640

    @pl.when(core_ref[0] == 0)
    def _():
        place(beside_ref, rows, out_ref)

    @pl.when(core_ref[0] != 0)
    def _():
        place(own_ref, rows, out_ref)

    lead = columns_ref[:, 0:1]
    pull = columns_ref[:, 1:2]
    total = jnp.zeros(values_ref.shape, F32)
    for j in range(width // tile):
        span = slice(tile * j, tile * (j + 1))
        slope = lead * weighted_ref[:, span] - pull * resid_ref[:, span].astype(F32)
        unit = (slope * scale_ref[:, span]).astype(BF16)
        unit_ref[:, span] = unit
        total = total + jnp.dot(unit, out_ref[span, :], preferred_element_type=F32)
    values_ref[...] = total * value_scale_ref[...]


def list_factor(arrived_ref, teacher_ref, segment_ref):
    stats = jnp.sum(arrived_ref[...], axis=0)
    lanes = lax.broadcasted_iota(jnp.int32, (1, 128), 1)
    real = lanes < CANDS
    counts = jnp.where(real, stats[1:2, :], 1.0)
    cand_score = jnp.where(real, stats[0:1, :] / counts, 0.0)
    teacher = teacher_ref[...]
    exp_teacher = jnp.where(real, jnp.exp(teacher), 0.0)
    exp_student = jnp.where(real, jnp.exp(cand_score), 0.0)
    log_teacher = teacher - jnp.log(jnp.sum(exp_teacher, axis=1, keepdims=True))
    log_student = cand_score - jnp.log(jnp.sum(exp_student, axis=1, keepdims=True))
    grad_cand = (jnp.exp(log_student) - jnp.exp(log_teacher)) / counts
    places = lax.broadcasted_iota(jnp.int32, (segment_ref.shape[0], 128), 1)
    member = segment_ref[...] == places
    factor = jnp.sum(jnp.where(member, grad_cand, 0.0), axis=1, keepdims=True)
    shares = jnp.exp(log_teacher) * (log_teacher - log_student)
    return factor, jnp.sum(jnp.where(real, shares, 0.0), axis=1, keepdims=True)


def term_kernel(
    pick_ref,
    normed_ref,
    unit_ref,
    values_ref,
    half_ref,
    arrived_ref,
    teacher_ref,
    segment_ref,
    term_ref,
    loss_ref,
    small_ref,
):
    @pl.when(pl.program_id(0) == 0)
    def _():
        factor, loss = list_factor(arrived_ref, teacher_ref, segment_ref)
        high = jnp.broadcast_to(loss, loss_ref.shape).astype(BF16).astype(F32)
        lanes = lax.broadcasted_iota(jnp.int32, loss_ref.shape, 1)
        low = jnp.where(lanes == 1, loss - high, 0.0)
        loss_ref[...] = jnp.where(lanes == 0, high, low)
        side = jnp.where(pick_ref[0] == 0, values_ref[...], half_ref[...].astype(F32))
        small_ref[...] = (factor * side).T.astype(BF16)

    def fill(tall_ref):
        term = jnp.dot(small_ref[...], tall_ref[...], preferred_element_type=F32)
        term_ref[...] = term.T.astype(term_ref.dtype)

    @pl.when(pick_ref[0] == 0)
    def _():
        fill(normed_ref)

    @pl.when(pick_ref[0] != 0)
    def _():
        fill(unit_ref)


def run_forward(core, hidden, root, own, beside, gain, scale, weighted, value_scale, segment):
    tokens, width = hidden.shape
    head = value_scale.shape[1]
    shape = jax.ShapeDtypeStruct
    vmem = pl.BlockSpec(memory_space=pltpu.VMEM)
    far = pl.BlockSpec(memory_space=pltpu.HBM)
    return pl.pallas_call(
        forward_kernel,
        out_shape=(
            shape((tokens, width), BF16),
            shape((tokens, width), BF16),
            shape((tokens, head), BF16),
            shape((tokens, 128), F32),
            shape((LIST_DEVICES, 8, 128), F32),
        ),
        in_specs=[pl.BlockSpec(memory_space=pltpu.SMEM), far] + [vmem] * 8,
        out_specs=(far, far, vmem, vmem, vmem),
        scratch_shapes=[
            pltpu.VMEM((width, head), BF16),
            pltpu.VMEM((width, head), BF16),
            pltpu.VMEM((tokens, width), BF16),
            pltpu.VMEM((tokens, width), BF16),
            pltpu.VMEM((tokens, width), BF16),
            pltpu.SemaphoreType.DMA((3, width // 640)),
        ],
        compiler_params=pltpu.CompilerParams(vmem_limit_bytes=VMEM_LIMIT),
        cost_estimate=pl.CostEstimate(
            flops=4 * tokens * width * head, bytes_accessed=12 * width * tokens, transcendentals=tokens
        ),
        name="forward",
    )(core, hidden, root, own, beside, gain, scale, weighted, value_scale, segment)


def run_backward(core, resid, own, beside, columns, scale, weighted, value_scale):
    tokens, width = resid.shape
    head = value_scale.shape[1]
    vmem = pl.BlockSpec(memory_space=pltpu.VMEM)
    return pl.pallas_call(
        backward_kernel,
        out_shape=(
            jax.ShapeDtypeStruct((tokens, width), BF16),
            jax.ShapeDtypeStruct((tokens, head), F32),
        ),
        in_specs=[pl.BlockSpec(memory_space=pltpu.SMEM)] + [vmem] * 7,
        out_specs=(vmem,) * 2,
        scratch_shapes=[pltpu.VMEM((width, head), BF16)],
        compiler_params=pltpu.CompilerParams(vmem_limit_bytes=VMEM_LIMIT),
        cost_estimate=pl.CostEstimate(
            flops=2 * tokens * width * head, bytes_accessed=8 * width * tokens, transcendentals=0
        ),
        name="backward",
    )(core, resid, own, beside, columns, scale, weighted, value_scale)


def run_term(pick, normed, unit, values, half, arrived, teacher, segment):
    tokens, width = normed.shape
    head = values.shape[1]
    tile = width // 2
    whole = lambda j, pick: (0, 0)
    return pl.pallas_call(
        term_kernel,
        out_shape=(
            jax.ShapeDtypeStruct((width, head), BF16),
            jax.ShapeDtypeStruct((8, 128), F32),
        ),
        grid_spec=pltpu.PrefetchScalarGridSpec(
            num_scalar_prefetch=1,
            grid=(width // tile,),
            in_specs=[
                pl.BlockSpec((tokens, tile), lambda j, pick: (0, j * (1 - pick[0]))),
                pl.BlockSpec((tokens, tile), lambda j, pick: (0, j * pick[0])),
                pl.BlockSpec((tokens, head), whole),
                pl.BlockSpec((tokens, head), whole),
                pl.BlockSpec(arrived.shape, lambda j, pick: (0, 0, 0)),
                pl.BlockSpec((1, 128), whole),
                pl.BlockSpec((tokens, 1), whole),
            ],
            out_specs=(
                pl.BlockSpec((tile, head), lambda j, pick: (j, 0)),
                pl.BlockSpec((8, 128), whole),
            ),
            scratch_shapes=[pltpu.VMEM((head, tokens), BF16)],
        ),
        compiler_params=pltpu.CompilerParams(vmem_limit_bytes=TERM_LIMIT),
        cost_estimate=pl.CostEstimate(
            flops=2 * tokens * width * head, bytes_accessed=4 * width * tokens, transcendentals=0
        ),
        name="term",
    )(pick, normed, unit, values, half, arrived, teacher, segment)


def shards(
    hidden,
    segment,
    grades,
    value_codes,
    value_scale,
    output_codes,
    output_scale,
    norm_gain,
    final_gain,
    score_vector,
):
    rows, head_size = value_codes.shape
    core = lax.axis_index("c")
    first = core == 0
    tokens = hidden[0]
    width = tokens.shape[1]
    seg_local = segment[0][:, None]

    with jax.named_scope("gather"):
        vectors = jnp.where(
            first, jnp.stack([norm_gain, output_scale]), jnp.stack([final_gain, score_vector])
        )
        vectors = jnp.pad(vectors, ((0, 6), (0, head_size - rows)))
        mine = jnp.concatenate([jnp.where(first, value_codes, output_codes), vectors], axis=0)
        other = lax.ppermute(mine, Z, half_partner())
        block = jnp.where(lax.axis_index("zh") == lax.axis_index("zb"), mine, other)
        column = lax.all_to_all(jnp.broadcast_to(block, (8,) + block.shape), Y, 0, 0)
        column = jnp.concatenate(
            [
                column[:, :rows].reshape(8 * rows, head_size),
                column[:, rows : rows + 2].reshape(16, head_size),
            ],
            axis=0,
        )
        spread = jnp.broadcast_to(column, (8,) + column.shape)
        own = lax.all_to_all(spread, XB, 0, 0)
        tokens32 = tokens.astype(F32)
        root = jnp.sqrt(jnp.mean(tokens32 * tokens32, axis=-1, keepdims=True) + EPSILON)
        beside = lax.ppermute(own, "c", SWAP)

        def vector(block, which):
            parts = block[:, 8 * rows :, :rows].reshape(8, 8, 2, rows)[:, :, which]
            return jnp.swapaxes(parts, 0, 1).reshape(1, width).astype(F32)

        gain32 = jnp.where(first, vector(own, 0), vector(beside, 0))
        scale32 = jnp.where(first, vector(own, 1), vector(beside, 1))
        final32 = jnp.where(first, vector(beside, 0), vector(own, 0))
        score32 = jnp.where(first, vector(beside, 1), vector(own, 1))
        weighted = final32 * score32

    value_row = value_scale[None, :]
    pick = core.astype(jnp.int32)[None]
    normed, resid, value_half, columns, stats = run_forward(
        pick, tokens, root, own, beside, gain32, scale32, weighted, value_row, seg_local
    )
    with jax.named_scope("stats"):
        arrived = lax.all_to_all(stats, ("yl", "x", "zh"), 0, 0)

    unit, values = run_backward(pick, resid, own, beside, columns, scale32, weighted, value_row)

    teacher = lax.dynamic_index_in_dim(grades[0], lax.axis_index("yh"), 0, keepdims=True)
    teacher = jnp.pad(teacher.astype(F32), ((0, 0), (0, head_size - CANDS)))

    give, loss_row = run_term(1 - pick, normed, unit, values, value_half, arrived, teacher, seg_local)
    with jax.named_scope("reduce"):
        got = lax.ppermute(give, "c", SWAP)
        keep, _ = run_term(pick, normed, unit, values, value_half, arrived, teacher, seg_local)
        both = (keep.astype(F32) + got.astype(F32)).astype(BF16)
        loss_row = jnp.broadcast_to(loss_row.astype(BF16), (8, 8, head_size))
        both, loss_row = lax.optimization_barrier((both, loss_row))
        half = rows // 2
        sent = both.reshape(8, 4, 2, 2, half, head_size).transpose(1, 3, 0, 2, 4, 5)
        came = lax.all_to_all(sent.reshape(8, 8 * rows, head_size), XB, 0, 0)
        part = jnp.sum(came.astype(F32), axis=0).astype(BF16).reshape(8, rows, head_size)
        part = jnp.concatenate([part, loss_row], axis=1)
        came = lax.all_to_all(part, Y, 0, 0)
        losses = came.reshape(4, 2, rows + 8, head_size)[:, 0, rows, :2]
        list_loss = jnp.sum(losses.astype(F32), axis=-1)
        part = jnp.sum(came[:, :rows].astype(F32), axis=0).astype(BF16)
        part, list_loss = lax.optimization_barrier((part, list_loss))
        part = part.reshape(2, 1, half, head_size)
        part = jnp.broadcast_to(part, (2, 6, half, head_size)).reshape(12, half, head_size)
        came = lax.all_to_all(part, Z, 0, 0).astype(F32)
        total = jnp.sum(came.reshape(6, 2, half, head_size), axis=0).reshape(rows, head_size)
        pair = lax.all_gather(total, "c")
    return (pair[0], pair[1], list_loss[None, :])


def solution(mesh):
    grid = Mesh(mesh.devices.reshape(4, 2, 4, 2, 3, 2, 2), WIDE + NARROW)
    in_specs = (
        P(NARROW, WIDE, None),
        P(NARROW, WIDE),
        P(NARROW, None, None),
        P(WIDE, None),
        P(),
        P(WIDE, None),
        P(WIDE),
        P(WIDE),
        P(WIDE),
        P(WIDE),
    )
    out_specs = (P(WIDE, None), P(WIDE, None), P(NARROW, None))
    return jax.shard_map(shards, mesh=grid, in_specs=in_specs, out_specs=out_specs, check_vma=False)
```
